256 devices in a mesh: dp: 4 (over x), ctx: 16 (over z, core), tp: 4 (over y).
Axes of the slice: x: 4, y: 4, z: 8, core: 2. Of those that a mesh axis runs over, the one named last changes fastest.
Arguments:
- signal: float32 [4, 2048, 2048], P('dp', 'tp', 'ctx'), may hold values from -6 to 6
- upstream: float32 [4, 2048, 2048], P('dp', 'tp', 'ctx'), may hold values from -6 to 6
- filter_taps: float32 [2048, 2048], P('tp', 'ctx'), may hold values from -5 to 5
- skip_gain: float32 [2048], P('tp'), may hold values from 0.5 to 1.5
Outputs:
- input_grad: float32 [4, 2048, 2048], P('dp', 'tp', 'ctx')
- filter_grad: float32 [2048, 2048], P('tp', 'ctx')
The draws below stay inside these ranges and needn't reach their ends.
All inputs are finite; a program needn't handle non-finite values.
Results may differ from the reference program's by a relative error of at most 0.00011.
Values sent between devices are 32-bit elements; how exact they have to be, the bound alone decides.
A program may use at most 64 MiB of HBM per device.

```python
import math
import jax
import jax.numpy as jnp
from jax import lax

CH = 2048
BATCH = 4
LENGTH = 2048


def draw_filter_taps(key, part):
    key = jax.random.fold_in(key, 11)
    rate_key, noise_key, level_key, sign_key, tail_key = jax.random.split(key, 5)
    low_end = math.log(16.0)
    high_end = math.log(4.0 * LENGTH)
    time_scale = jnp.exp(jax.random.uniform(rate_key, (CH, 1), jnp.float32, low_end, high_end))
    steps_axis = jnp.arange(LENGTH, dtype=jnp.float32)[None, :]
    envelope = jnp.exp(-steps_axis / time_scale) * jnp.sqrt(1.0 - jnp.exp(-2.0 / time_scale))
    noise_part = jnp.clip(jax.random.normal(noise_key, (CH, LENGTH), jnp.float32), -4.0, 4.0)
    tail_level = jnp.exp(jax.random.uniform(level_key, (CH, 1), jnp.float32, math.log(0.0002), math.log(0.0008)))
    tail_sign = jax.random.randint(sign_key, (CH, 1), 0, 2).astype(jnp.float32) * 2.0 - 1.0
    tail_rough = jax.random.uniform(tail_key, (CH, LENGTH), jnp.float32, 0.5, 1.5)
    tail_part = tail_sign * tail_level * tail_rough
    return (noise_part * envelope + tail_part).astype(jnp.float32)


def level_of(key, dims, pieces, smallest, high):
    loudness = 1.0
    for position, parts in pieces:
        draws = jax.random.uniform(jax.random.fold_in(jax.random.fold_in(key, 6), position), (parts,), jnp.float32, smallest / len(pieces), high / len(pieces))
        loudness = loudness * jnp.repeat(jnp.exp(draws), dims[position] // parts).reshape((-1,) + (1,) * (len(dims) - 1 - position))
    return loudness


def normal_values(rng, shape, scale, bound, pieces=(), held_as=jnp.bfloat16):
    factor_of = level_of(rng, shape, pieces, -0.22, 0.18) if pieces else 1.0
    drawn = jax.random.normal(rng, shape, jnp.float32) * scale * factor_of
    return jnp.minimum(jnp.maximum(drawn, -bound), bound).astype(held_as)


def setup_inputs(seed: int = 0) -> dict:
    arg_keys = jax.random.split(jax.random.key(seed), 5)
    return {
        "signal": normal_values(arg_keys[0], (BATCH, CH, LENGTH), 1.0, 6.0, ((0, 4), (1, 4), (2, 16)), jnp.float32),
        "upstream": normal_values(arg_keys[1], (BATCH, CH, LENGTH), 1.0, 6.0, ((0, 4), (1, 4), (2, 16)), jnp.float32),
        "filter_taps": draw_filter_taps(jax.random.fold_in(arg_keys[4], 71), 0),
        "skip_gain": jnp.clip(0.5 + 1.0 * jax.random.uniform(arg_keys[3], (CH,), jnp.float32) ** level_of(arg_keys[3], (CH,), ((0, 4),), -0.2, 0.2), 0.5, 1.5),
    }


def reference(signal, upstream, filter_taps, skip_gain):
    padded = 2 * LENGTH
    signal_spec = jnp.fft.rfft(signal, n=padded, axis=-1)
    filter_spec = jnp.fft.rfft(filter_taps, n=padded, axis=-1)
    upstream_spec = jnp.fft.rfft(upstream, n=padded, axis=-1)
    through = jnp.fft.irfft(upstream_spec * jnp.conj(filter_spec)[None], n=padded, axis=-1)[..., :LENGTH]
    input_grad = through + skip_gain[None, :, None] * upstream
    per_sequence = jnp.fft.irfft(upstream_spec * jnp.conj(signal_spec), n=padded, axis=-1)[..., :LENGTH]
    filter_grad = lax.optimization_barrier(jnp.sum(per_sequence, axis=0)) / math.sqrt(BATCH * LENGTH)
    return (input_grad.astype(jnp.float32), filter_grad.astype(jnp.float32))
```

```python
import functools
import math

import jax
import jax.numpy as jnp
import numpy as np
from jax import lax
from jax.experimental import pallas as pl
from jax.experimental.pallas import tpu as pltpu
from jax.sharding import PartitionSpec as P

SUB = 8
LANES = 128
BLOCKS = 16
FOLD = 2 * BLOCKS
KEPT = BLOCKS + 1
FULL = FOLD * LANES


def turn(value, step, modulus):
    re, im = value
    step %= modulus
    if step == 0:
        return value
    if 2 * step == modulus:
        return (-re, -im)
    if 4 * step == modulus:
        return (-im, re)
    if 4 * step == 3 * modulus:
        return (im, -re)
    if 8 * step % modulus == 0:
        root = math.sqrt(0.5)
        odd = 8 * step // modulus
        plus, minus = (re + im) * root, (re - im) * root
        if odd == 1:
            return (minus, plus)
        if odd == 3:
            return (-plus, minus)
        if odd == 5:
            return (-minus, -plus)
        return (plus, -minus)
    angle = 2.0 * math.pi * step / modulus
    c, s = math.cos(angle), math.sin(angle)
    return (re * c - im * s, re * s + im * c)


def add(left, right):
    return (left[0] + right[0], left[1] + right[1])


def sub(left, right):
    return (left[0] - right[0], left[1] - right[1])


def dft(values, sign):
    size = len(values)
    if size == 1:
        return values
    even = dft(values[0::2], sign)
    odd = dft(values[1::2], sign)
    odd = [turn(value, sign * k, size) for k, value in enumerate(odd)]
    return [add(e, o) for e, o in zip(even, odd)] + [sub(e, o) for e, o in zip(even, odd)]


def odd_forward(values):
    size = len(values)
    half = size // 2
    if size == 1:
        return {1: (values[0], None)}
    pairs = [turn((values[a], -values[a + half]), -a, 2 * size) for a in range(half)]
    result = {}
    for r, value in enumerate(dft(pairs, -1)):
        k = 4 * r + 1
        if k <= size:
            result[k] = value
        else:
            result[2 * size - k] = (value[0], -value[1])
    return result


def real_forward(values):
    size = len(values)
    if size == 1:
        return {0: (values[0], None)}
    half = size // 2
    sums = [values[a] + values[a + half] for a in range(half)]
    gaps = [values[a] - values[a + half] for a in range(half)]
    result = {2 * k: value for k, value in real_forward(sums).items()}
    result.update(odd_forward(gaps))
    return result


def padded_forward(values):
    result = {2 * k: value for k, value in real_forward(values).items()}
    result.update(odd_forward(values))
    return [result[k] for k in range(len(values) + 1)]


def odd_inverse(spec, size):
    half = size // 2
    if size == 1:
        return [spec[1][0]]
    inputs = []
    for r in range(half):
        k = 4 * r + 1
        if k <= size:
            inputs.append(spec[k])
        else:
            inputs.append((spec[2 * size - k][0], -spec[2 * size - k][1]))
    turned = [turn(value, a, 2 * size) for a, value in enumerate(dft(inputs, 1))]
    return [value[0] for value in turned] + [-value[1] for value in turned]


def real_inverse(spec, size):
    if size == 1:
        return [spec[0][0]]
    half = size // 2
    even = real_inverse({k // 2: v for k, v in spec.items() if k % 2 == 0}, half)
    odd = odd_inverse({k: v for k, v in spec.items() if k % 2 == 1}, half)
    return [e + o for e, o in zip(even, odd)] + [e - o for e, o in zip(even, odd)]


def padded_inverse(spec):
    half = len(spec) - 1
    even = real_inverse({k // 2: spec[k] for k in range(0, half + 1, 2)}, half)
    odd = odd_inverse({k: spec[k] for k in range(1, half + 1, 2)}, half)
    return [e + o for e, o in zip(even, odd)]


def split(value):
    high = value.astype(jnp.bfloat16)
    low = (value - high.astype(jnp.float32)).astype(jnp.bfloat16)
    return high, low


def tables():
    lane = np.arange(LANES)
    angle = 2.0 * np.pi * (np.outer(lane, lane) % LANES) / LANES
    c, s = np.cos(angle), np.sin(angle)
    forward = np.block([[c, -s], [s, c]])
    inverse = np.block([[c, s], [-s, c]])
    matrices = []
    for matrix in (forward, inverse):
        matrix = matrix.astype(np.float32)
        high = matrix.astype(jnp.bfloat16)
        low = (matrix - high.astype(np.float32)).astype(jnp.bfloat16)
        matrices += [high, low]
    angle = 2.0 * np.pi * np.outer(np.arange(KEPT), lane) / FULL
    scale = np.full((KEPT, 1), 2.0 / FULL)
    scale[0] = scale[-1] = 1.0 / FULL
    rows = [np.cos(angle), -np.sin(angle), np.cos(angle) * scale, np.sin(angle) * scale]
    twist = np.stack(rows, 1)[:, :, None, :]
    twist = np.broadcast_to(twist, (KEPT, 4, SUB, LANES)).astype(np.float32)
    return np.stack(matrices), twist


def product(value, matrix_ref, index):
    high, low = split(value)
    big, small = matrix_ref[index], matrix_ref[index + 1]
    dot = functools.partial(jnp.dot, preferred_element_type=jnp.float32)
    return dot(high, big) + (dot(high, small) + dot(low, big))


def kernel(
    seqs, places,
    up_ref, sig_ref, taps_ref, matrix_ref, twist_ref,
    ig_ref, fg_ref,
    up_buf, sig_buf, taps_buf, ig_buf, fg_buf, mid, up_spec, taps_spec, work,
    send_sem, recv_sem,
):
    row, col = lax.axis_index("dp"), lax.axis_index("ctx")
    group = row * places + col
    peers = seqs * places

    def target(step):
        r = lax.rem(row + step // places, seqs)
        c = lax.rem(col + step % places, places)
        return r, c

    def tile(index):
        return pl.ds(pl.multiple_of(index * SUB, SUB), SUB)

    barrier = pltpu.get_barrier_semaphore()

    def greet(step, carry):
        r, c = target(step)
        pl.semaphore_signal(
            barrier, inc=1, device_id={"dp": r, "ctx": c}, device_id_type=pl.DeviceIdType.MESH
        )
        return carry

    lax.fori_loop(1, peers, greet, 0)
    pl.semaphore_wait(barrier, peers - 1)

    def push(src, dst, kind, r, c):
        pltpu.make_async_remote_copy(
            src_ref=src,
            dst_ref=dst,
            send_sem=send_sem.at[kind],
            recv_sem=recv_sem.at[kind],
            device_id={"dp": r, "ctx": c},
            device_id_type=pl.DeviceIdType.MESH,
        ).start()

    def send_taps(step, carry):
        c = lax.rem(col + step, places)
        push(taps_ref.at[tile(row * places + c)], taps_buf.at[col], 1, row, c)
        return carry

    def send_from(ref, buf, kind):
        def body(step, carry):
            r, c = target(step)
            push(ref.at[tile(r * places + c)], buf.at[row, col], kind, r, c)
            return carry

        return body

    pltpu.make_async_copy(up_ref.at[tile(group)], up_buf.at[row, col], recv_sem.at[0]).start()
    pltpu.make_async_copy(taps_ref.at[tile(group)], taps_buf.at[col], recv_sem.at[1]).start()
    pltpu.make_async_copy(sig_ref.at[tile(group)], sig_buf.at[row, col], recv_sem.at[2]).start()
    lax.fori_loop(1, places, send_taps, 0)
    lax.fori_loop(1, peers, send_from(up_ref, up_buf, 0), 0)
    lax.fori_loop(1, peers, send_from(sig_ref, sig_buf, 2), 0)

    def arrived(ref, kind):
        pltpu.make_async_copy(ref, ref, recv_sem.at[kind]).wait()

    def left(ref, kind, count):
        part = ref.at[pl.ds(0, count * SUB)]
        pltpu.make_async_copy(part, part, send_sem.at[kind]).wait()

    def fold(load, store):
        spec = padded_forward([load(a) for a in range(BLOCKS)])
        for k, (re, im) in enumerate(spec):
            c, s = twist_ref[k, 0], twist_ref[k, 1]
            if im is None:
                store(k, re * c, re * s)
            else:
                store(k, re * c - im * s, re * s + im * c)

    def unfold(load):
        spec = []
        for k in range(KEPT):
            re, im = load(k)
            c, s = twist_ref[k, 2], twist_ref[k, 3]
            spec.append((re * c - im * s, re * s + im * c))
        return padded_inverse(spec)

    def fold_all(buf):
        def body(b, carry):
            def store(k, re, im):
                mid[k, b, :, :LANES] = re
                mid[k, b, :, LANES:] = im

            fold(lambda a: buf[b, a], store)
            return carry

        lax.fori_loop(0, seqs, body, 0)

    whole = (KEPT * seqs * SUB, 2 * LANES)
    shaped = (KEPT, seqs, SUB, 2 * LANES)

    arrived(taps_buf, 1)

    def store_taps(k, re, im):
        work[k, :, :LANES] = re
        work[k, :, LANES:] = im

    fold(lambda a: taps_buf[a], store_taps)
    taps_spec[...] = product(work[...].reshape(KEPT * SUB, 2 * LANES), matrix_ref, 0).reshape(
        KEPT, SUB, 2 * LANES
    )

    arrived(up_buf, 0)
    fold_all(up_buf)
    up_spec[...] = product(mid[...].reshape(whole), matrix_ref, 0).reshape(shaped)

    def times_taps(k, carry):
        fr, fi = taps_spec[k, :, :LANES], taps_spec[k, :, LANES:]
        for b in range(seqs):
            ur, ui = up_spec[k, b, :, :LANES], up_spec[k, b, :, LANES:]
            mid[k, b, :, :LANES] = ur * fr + ui * fi
            mid[k, b, :, LANES:] = ui * fr - ur * fi
        return carry

    lax.fori_loop(0, KEPT, times_taps, 0)
    mid[...] = product(mid[...].reshape(whole), matrix_ref, 2).reshape(shaped)

    def unfold_input(b, carry):
        values = unfold(lambda k: (mid[k, b, :, :LANES], mid[k, b, :, LANES:]))
        for a in range(BLOCKS):
            ig_buf[b, a] = values[a]
        return carry

    lax.fori_loop(0, seqs, unfold_input, 0)

    def send_back(src, dst, kind):
        def body(step, carry):
            r, c = target(step)
            push(src(r, c), dst.at[tile(group)], kind, r, c)
            return carry

        pltpu.make_async_copy(src(row, col), dst.at[tile(group)], recv_sem.at[kind]).start()
        lax.fori_loop(1, peers, body, 0)

    send_back(lambda r, c: ig_buf.at[r, c], ig_ref, 3)

    arrived(sig_buf, 2)
    fold_all(sig_buf)
    mid[...] = product(mid[...].reshape(whole), matrix_ref, 0).reshape(shaped)

    def times_signal(k, carry):
        re = im = 0.0
        for b in range(seqs):
            ur, ui = up_spec[k, b, :, :LANES], up_spec[k, b, :, LANES:]
            sr, si = mid[k, b, :, :LANES], mid[k, b, :, LANES:]
            re += ur * sr + ui * si
            im += ui * sr - ur * si
        work[k, :, :LANES] = re
        work[k, :, LANES:] = im
        return carry

    lax.fori_loop(0, KEPT, times_signal, 0)
    work[...] = product(work[...].reshape(KEPT * SUB, 2 * LANES), matrix_ref, 2).reshape(
        KEPT, SUB, 2 * LANES
    )
    values = unfold(lambda k: (work[k, :, :LANES], work[k, :, LANES:]))
    for a in range(BLOCKS):
        fg_buf[a] = values[a]
    send_back(lambda r, c: fg_buf.at[c], fg_ref, 4)

    left(taps_ref, 1, places - 1)
    left(up_ref, 0, peers - 1)
    left(sig_ref, 2, peers - 1)
    left(ig_ref, 3, peers - 1)
    left(fg_ref, 4, peers - 1)
    arrived(ig_ref, 3)
    arrived(fg_ref, 4)


def shards(signal, upstream, filter_taps, skip_gain):
    seqs, places = lax.axis_size("dp"), lax.axis_size("ctx")
    channels, length = filter_taps.shape
    assert (channels, length, places) == (SUB * seqs * places, LANES, BLOCKS)
    matrices, twist = tables()
    rows = (channels, length)
    anywhere = pl.BlockSpec(memory_space=pl.ANY)
    vmem = pl.BlockSpec(memory_space=pltpu.VMEM)
    spec_shape = (KEPT, seqs, SUB, 2 * LANES)
    input_part, filter_part = pl.pallas_call(
        functools.partial(kernel, seqs, places),
        out_shape=[jax.ShapeDtypeStruct(rows, jnp.float32)] * 2,
        in_specs=[anywhere] * 3 + [vmem] * 2,
        out_specs=[anywhere] * 2,
        scratch_shapes=[
            pltpu.VMEM((seqs, places, SUB, LANES), jnp.float32),
            pltpu.VMEM((seqs, places, SUB, LANES), jnp.float32),
            pltpu.VMEM((places, SUB, LANES), jnp.float32),
            pltpu.VMEM((seqs, places, SUB, LANES), jnp.float32),
            pltpu.VMEM((places, SUB, LANES), jnp.float32),
            pltpu.VMEM(spec_shape, jnp.float32),
            pltpu.VMEM(spec_shape, jnp.float32),
            pltpu.VMEM((KEPT, SUB, 2 * LANES), jnp.float32),
            pltpu.VMEM((KEPT, SUB, 2 * LANES), jnp.float32),
            pltpu.SemaphoreType.DMA((5,)),
            pltpu.SemaphoreType.DMA((5,)),
        ],
        compiler_params=pltpu.CompilerParams(
            collective_id=0, has_side_effects=True, vmem_limit_bytes=32 * 1024 * 1024
        ),
    )(
        upstream[0],
        signal[0],
        filter_taps,
        jnp.asarray(matrices),
        jnp.asarray(twist),
    )
    input_grad = (input_part + skip_gain[:, None] * upstream[0])[None]
    filter_grad = filter_part * (1.0 / math.sqrt(seqs * places * length))
    return (input_grad, filter_grad)


def solution(mesh):
    placed = (P("dp", "tp", "ctx"), P("dp", "tp", "ctx"), P("tp", "ctx"), P("tp"))
    return jax.shard_map(
        shards,
        mesh=mesh,
        in_specs=placed,
        out_specs=(P("dp", "tp", "ctx"), P("tp", "ctx")),
        check_vma=False,
    )
```

```python
import functools
import math

import jax
import jax.numpy as jnp
import numpy as np
from jax import lax
from jax.experimental import pallas as pl
from jax.experimental.pallas import tpu as pltpu
from jax.sharding import PartitionSpec as P

SUB = 8
LANES = 128
BLOCKS = 16
FOLD = 2 * BLOCKS
KEPT = BLOCKS + 1
FULL = FOLD * LANES


def turn(value, step, modulus):
    re, im = value
    step %= modulus
    if step == 0:
        return value
    if 2 * step == modulus:
        return (-re, -im)
    if 4 * step == modulus:
        return (-im, re)
    if 4 * step == 3 * modulus:
        return (im, -re)
    if 8 * step % modulus == 0:
        root = math.sqrt(0.5)
        odd = 8 * step // modulus
        plus, minus = (re + im) * root, (re - im) * root
        if odd == 1:
            return (minus, plus)
        if odd == 3:
            return (-plus, minus)
        if odd == 5:
            return (-minus, -plus)
        return (plus, -minus)
    angle = 2.0 * math.pi * step / modulus
    c, s = math.cos(angle), math.sin(angle)
    return (re * c - im * s, re * s + im * c)


def add(left, right):
    return (left[0] + right[0], left[1] + right[1])


def sub(left, right):
    return (left[0] - right[0], left[1] - right[1])


def dft(values, sign):
    size = len(values)
    if size == 1:
        return values
    even = dft(values[0::2], sign)
    odd = dft(values[1::2], sign)
    odd = [turn(value, sign * k, size) for k, value in enumerate(odd)]
    return [add(e, o) for e, o in zip(even, odd)] + [sub(e, o) for e, o in zip(even, odd)]


def odd_forward(values):
    size = len(values)
    half = size // 2
    if size == 1:
        return {1: (values[0], None)}
    pairs = [turn((values[a], -values[a + half]), -a, 2 * size) for a in range(half)]
    result = {}
    for r, value in enumerate(dft(pairs, -1)):
        k = 4 * r + 1
        if k <= size:
            result[k] = value
        else:
            result[2 * size - k] = (value[0], -value[1])
    return result


def real_forward(values):
    size = len(values)
    if size == 1:
        return {0: (values[0], None)}
    half = size // 2
    sums = [values[a] + values[a + half] for a in range(half)]
    gaps = [values[a] - values[a + half] for a in range(half)]
    result = {2 * k: value for k, value in real_forward(sums).items()}
    result.update(odd_forward(gaps))
    return result


def padded_forward(values):
    result = {2 * k: value for k, value in real_forward(values).items()}
    result.update(odd_forward(values))
    return [result[k] for k in range(len(values) + 1)]


def odd_inverse(spec, size):
    half = size // 2
    if size == 1:
        return [spec[1][0]]
    inputs = []
    for r in range(half):
        k = 4 * r + 1
        if k <= size:
            inputs.append(spec[k])
        else:
            inputs.append((spec[2 * size - k][0], -spec[2 * size - k][1]))
    turned = [turn(value, a, 2 * size) for a, value in enumerate(dft(inputs, 1))]
    return [value[0] for value in turned] + [-value[1] for value in turned]


def real_inverse(spec, size):
    if size == 1:
        return [spec[0][0]]
    half = size // 2
    even = real_inverse({k // 2: v for k, v in spec.items() if k % 2 == 0}, half)
    odd = odd_inverse({k: v for k, v in spec.items() if k % 2 == 1}, half)
    return [e + o for e, o in zip(even, odd)] + [e - o for e, o in zip(even, odd)]


def padded_inverse(spec):
    half = len(spec) - 1
    even = real_inverse({k // 2: spec[k] for k in range(0, half + 1, 2)}, half)
    odd = odd_inverse({k: spec[k] for k in range(1, half + 1, 2)}, half)
    return [e + o for e, o in zip(even, odd)]


def split(value):
    high = value.astype(jnp.bfloat16)
    low = (value - high.astype(jnp.float32)).astype(jnp.bfloat16)
    return high, low


def tables():
    lane = np.arange(LANES)
    angle = 2.0 * np.pi * (np.outer(lane, lane) % LANES) / LANES
    c, s = np.cos(angle), np.sin(angle)
    forward = np.block([[c, -s], [s, c]])
    inverse = np.block([[c, s], [-s, c]])
    matrices = []
    for matrix in (forward, inverse):
        matrix = matrix.astype(np.float32)
        high = matrix.astype(jnp.bfloat16)
        low = (matrix - high.astype(np.float32)).astype(jnp.bfloat16)
        matrices += [high, low]
    angle = 2.0 * np.pi * np.outer(np.arange(KEPT), lane) / FULL
    scale = np.full((KEPT, 1), 2.0 / FULL)
    scale[0] = scale[-1] = 1.0 / FULL
    rows = [np.cos(angle), -np.sin(angle), np.cos(angle) * scale, np.sin(angle) * scale]
    twist = np.stack(rows, 1)[:, :, None, :]
    twist = np.broadcast_to(twist, (KEPT, 4, SUB, LANES)).astype(np.float32)
    return np.stack(matrices), twist


def product(value, matrix_ref, index):
    high, low = split(value)
    big, small = matrix_ref[index], matrix_ref[index + 1]
    dot = functools.partial(jnp.dot, preferred_element_type=jnp.float32)
    return dot(high, big) + (dot(high, small) + dot(low, big))


def kernel(
    seqs, places,
    up_hbm, sig_hbm, taps_hbm, gain_hbm, matrix_hbm, twist_hbm,
    ig_ref, fg_ref,
    up_buf, sig_buf, taps_buf, ig_buf, fg_buf, mid, up_spec, taps_spec, work,
    gain_ref, matrix_ref, twist_ref, up_here, sig_here, taps_here,
    send_sem, recv_sem, table_sem, ready,
):
    row, col = lax.axis_index("dp"), lax.axis_index("ctx")
    group = row * places + col
    peers = seqs * places

    def tile(index):
        return pl.ds(pl.multiple_of(index * SUB, SUB), SUB)

    ahead = [
        (taps_hbm, taps_here),
        (up_hbm, up_here),
        (sig_hbm, sig_here),
        (gain_hbm, gain_ref),
        (matrix_hbm, matrix_ref),
        (twist_hbm, twist_ref),
    ]
    ahead = [pltpu.make_async_copy(src, dst, table_sem.at[i]) for i, (src, dst) in enumerate(ahead)]
    for copy in ahead:
        copy.start()

    barrier = pltpu.get_barrier_semaphore()

    def signal(semaphore, r, c):
        pl.semaphore_signal(
            semaphore, inc=1, device_id={"dp": r, "ctx": c}, device_id_type=pl.DeviceIdType.MESH
        )

    def along(shift):
        return lax.rem(row + shift, seqs)

    def across(shift):
        return lax.rem(col + shift, places)

    for shift in range(1, seqs):
        signal(barrier, along(shift), col)
    for shift in range(1, places):
        signal(barrier, row, across(shift))
    pl.semaphore_wait(barrier, seqs + places - 2)
    for shift in range(1, seqs):
        signal(ready, along(shift), col)

    def push(src, dst, kind, r, c):
        pltpu.make_async_remote_copy(
            src_ref=src,
            dst_ref=dst,
            send_sem=send_sem.at[kind],
            recv_sem=recv_sem.at[kind],
            device_id={"dp": r, "ctx": c},
            device_id_type=pl.DeviceIdType.MESH,
        ).start()

    def shift_of(step):
        return places // 2 + (step + 1) // 2 * (1 - 2 * lax.rem(step, 2))

    def send(src, dst, kind, *turns, own=None):
        def body(step, carry):
            shift = shift_of(step)
            c = across(shift)
            for turn in turns:
                r = along(turn) if turn else row
                push(src(r, c), dst, kind if own is None else own + shift, r, c)
            return carry

        lax.fori_loop(0, places - (0 in turns), body, 0)

    def stay(src, dst, kind):
        pltpu.make_async_copy(src, dst, recv_sem.at[kind]).start()

    def slab(ref):
        return lambda r, c: ref.at[tile(r * places + c)]

    ahead[0].wait()
    stay(slab(taps_here)(row, col), taps_buf.at[col], 1)
    send(slab(taps_here), taps_buf.at[col], 1, 0)
    ahead[1].wait()
    stay(slab(up_here)(row, col), up_buf.at[row, col], 0)
    send(slab(up_here), up_buf.at[row, col], 0, 0)
    pl.semaphore_wait(ready, seqs - 1)
    send(slab(up_here), up_buf.at[row, col], 0, 2, 1, 3)
    ahead[2].wait()
    stay(slab(sig_here)(row, col), sig_buf.at[row, col], 2)
    send(slab(sig_here), sig_buf.at[row, col], 2, 2, 1, 3)
    send(slab(sig_here), sig_buf.at[row, col], 2, 0)

    def arrived(ref, kind):
        pltpu.make_async_copy(ref, ref, recv_sem.at[kind]).wait()

    def left(ref, kind, count):
        part = ref.at[pl.ds(0, count * SUB)]
        pltpu.make_async_copy(part, part, send_sem.at[kind]).wait()

    def fold(load, store):
        spec = padded_forward([load(a) for a in range(BLOCKS)])
        for k, (re, im) in enumerate(spec):
            c, s = twist_ref[k, 0], twist_ref[k, 1]
            if im is None:
                store(k, re * c, re * s)
            else:
                store(k, re * c - im * s, re * s + im * c)

    def unfold(load):
        spec = []
        for k in range(KEPT):
            re, im = load(k)
            c, s = twist_ref[k, 2], twist_ref[k, 3]
            spec.append((re * c - im * s, re * s + im * c))
        return padded_inverse(spec)

    def fold_all(buf):
        def body(b, carry):
            def store(k, re, im):
                mid[k, b, :, :LANES] = re
                mid[k, b, :, LANES:] = im

            fold(lambda a: buf[b, a], store)
            return carry

        lax.fori_loop(0, seqs, body, 0)

    whole = (KEPT * seqs * SUB, 2 * LANES)
    shaped = (KEPT, seqs, SUB, 2 * LANES)

    for copy in ahead[3:]:
        copy.wait()
    lane = lax.broadcasted_iota(jnp.int32, (SUB, LANES), 1)
    channel = lax.broadcasted_iota(jnp.int32, (SUB, LANES), 0) + col * SUB
    gain = jnp.where(lane == channel, gain_ref[pl.ds(row, 1), :], 0.0)
    gain = jnp.sum(gain, axis=1, keepdims=True)

    arrived(taps_buf, 1)

    def store_taps(k, re, im):
        work[k, :, :LANES] = re
        work[k, :, LANES:] = im

    fold(lambda a: taps_buf[a], store_taps)
    taps_spec[...] = product(work[...].reshape(KEPT * SUB, 2 * LANES), matrix_ref, 0).reshape(
        KEPT, SUB, 2 * LANES
    )

    arrived(up_buf, 0)
    fold_all(up_buf)
    up_spec[...] = product(mid[...].reshape(whole), matrix_ref, 0).reshape(shaped)

    def times_taps(k, carry):
        fr, fi = taps_spec[k, :, :LANES], taps_spec[k, :, LANES:]
        for b in range(seqs):
            ur, ui = up_spec[k, b, :, :LANES], up_spec[k, b, :, LANES:]
            mid[k, b, :, :LANES] = ur * fr + ui * fi
            mid[k, b, :, LANES:] = ui * fr - ur * fi
        return carry

    lax.fori_loop(0, KEPT, times_taps, 0)
    mid[...] = product(mid[...].reshape(whole), matrix_ref, 2).reshape(shaped)

    def unfold_input(b, carry):
        values = unfold(lambda k: (mid[k, b, :, :LANES], mid[k, b, :, LANES:]))
        for a in range(BLOCKS):
            ig_buf[b, a] = values[a] + gain * up_buf[b, a]
        return carry

    lax.fori_loop(0, seqs, unfold_input, 0)

    def send_input(*turns):
        send(lambda r, c: ig_buf.at[r, c], ig_ref.at[tile(group)], 3, *turns)

    stay(ig_buf.at[row, col], ig_ref.at[tile(group)], 3)
    left(sig_here, 2, peers - 1)
    send_input(2, 1)

    arrived(sig_buf, 2)
    fold_all(sig_buf)
    mid[...] = product(mid[...].reshape(whole), matrix_ref, 0).reshape(shaped)

    def times_signal(k, carry):
        re = im = 0.0
        for b in range(seqs):
            ur, ui = up_spec[k, b, :, :LANES], up_spec[k, b, :, LANES:]
            sr, si = mid[k, b, :, :LANES], mid[k, b, :, LANES:]
            re += ur * sr + ui * si
            im += ui * sr - ur * si
        work[k, :, :LANES] = re
        work[k, :, LANES:] = im
        return carry

    lax.fori_loop(0, KEPT, times_signal, 0)
    work[...] = product(work[...].reshape(KEPT * SUB, 2 * LANES), matrix_ref, 2).reshape(
        KEPT, SUB, 2 * LANES
    )
    values = unfold(lambda k: (work[k, :, :LANES], work[k, :, LANES:]))
    for a in range(BLOCKS):
        fg_buf[a] = values[a] * (1.0 / math.sqrt(seqs * places * LANES))
    first = 6
    send(lambda r, c: fg_buf.at[c], fg_ref.at[tile(group)], 4, 0, own=first)
    pltpu.make_async_copy(fg_buf.at[col], fg_ref.at[tile(group)], recv_sem.at[4]).start()
    send_input(3)
    send_input(0)

    def spread(part):
        for turn in (2, 1, 3):
            push(part, part, 5, along(turn), col)

    def pass_on(step, carry):
        shift = shift_of(places - 1 - step)
        part = fg_ref.at[tile(row * places + across(places - shift))]
        arrived(part, first + shift)
        spread(part)
        return carry

    part = fg_ref.at[tile(group)]
    arrived(part, 4)
    spread(part)
    lax.fori_loop(1, places, pass_on, 0)

    left(taps_here, 1, places - 1)
    left(up_here, 0, peers - 1)
    left(ig_ref, 3, peers - 1)
    part = fg_ref.at[tile(0)]
    for shift in range(1, places):
        pltpu.make_async_copy(part, part, send_sem.at[first + shift]).wait()
    left(fg_ref, 5, (seqs - 1) * places)
    arrived(ig_ref, 3)
    arrived(fg_ref.at[pl.ds(0, (seqs - 1) * places * SUB)], 5)


def deliver(ig_part, fg_part, ig_ref, fg_ref, sem):
    copies = [
        pltpu.make_async_copy(ig_part, ig_ref, sem.at[0]),
        pltpu.make_async_copy(fg_part, fg_ref, sem.at[1]),
    ]
    for copy in copies:
        copy.start()
    for copy in copies:
        copy.wait()


def shards(signal, upstream, filter_taps, skip_gain):
    seqs, places = lax.axis_size("dp"), lax.axis_size("ctx")
    channels, length = filter_taps.shape
    assert (channels, length, places) == (SUB * seqs * places, LANES, BLOCKS)
    assert places * SUB == LANES
    matrices, twist = tables()
    rows = (channels, length)
    hbm = pl.BlockSpec(memory_space=pltpu.HBM)
    vmem = pl.BlockSpec(memory_space=pltpu.VMEM)
    spec_shape = (KEPT, seqs, SUB, 2 * LANES)
    results = [pltpu.VMEM(rows, jnp.float32)] * 2
    parts = pl.pallas_call(
        functools.partial(kernel, seqs, places),
        out_shape=results,
        in_specs=[hbm] * 6,
        out_specs=[vmem] * 2,
        scratch_shapes=[
            pltpu.VMEM((seqs, places, SUB, LANES), jnp.float32),
            pltpu.VMEM((seqs, places, SUB, LANES), jnp.float32),
            pltpu.VMEM((places, SUB, LANES), jnp.float32),
            pltpu.VMEM((seqs, places, SUB, LANES), jnp.float32),
            pltpu.VMEM((places, SUB, LANES), jnp.float32),
            pltpu.VMEM(spec_shape, jnp.float32),
            pltpu.VMEM(spec_shape, jnp.float32),
            pltpu.VMEM((KEPT, SUB, 2 * LANES), jnp.float32),
            pltpu.VMEM((KEPT, SUB, 2 * LANES), jnp.float32),
            pltpu.VMEM((seqs, LANES), jnp.float32),
            pltpu.VMEM(matrices.shape, jnp.bfloat16),
            pltpu.VMEM(twist.shape, jnp.float32),
            pltpu.VMEM(rows, jnp.float32),
            pltpu.VMEM(rows, jnp.float32),
            pltpu.VMEM(rows, jnp.float32),
            pltpu.SemaphoreType.DMA((6 + places,)),
            pltpu.SemaphoreType.DMA((6 + places,)),
            pltpu.SemaphoreType.DMA((6,)),
            pltpu.SemaphoreType.REGULAR,
        ],
        compiler_params=pltpu.CompilerParams(
            collective_id=0, has_side_effects=True, vmem_limit_bytes=32 * 1024 * 1024
        ),
    )(
        *[
            pltpu.with_memory_space_constraint(value, pltpu.HBM)
            for value in (
                upstream[0],
                signal[0],
                filter_taps,
                skip_gain.reshape(seqs, LANES),
                jnp.asarray(matrices),
                jnp.asarray(twist),
            )
        ]
    )
    input_grad, filter_grad = pl.pallas_call(
        deliver,
        out_shape=[pltpu.HBM(rows, jnp.float32)] * 2,
        in_specs=[vmem] * 2,
        out_specs=[hbm] * 2,
        scratch_shapes=[pltpu.SemaphoreType.DMA((2,))],
    )(*[pltpu.with_memory_space_constraint(part, pltpu.VMEM) for part in parts])
    return (input_grad[None], filter_grad)


def solution(mesh):
    placed = (P("dp", "tp", "ctx"), P("dp", "tp", "ctx"), P("tp", "ctx"), P("tp"))
    return jax.shard_map(
        shards,
        mesh=mesh,
        in_specs=placed,
        out_specs=(P("dp", "tp", "ctx"), P("tp", "ctx")),
        check_vma=False,
    )
```

```python
import functools
import math

import jax
import jax.numpy as jnp
import numpy as np
from jax import lax
from jax.experimental import pallas as pl
from jax.experimental.pallas import tpu as pltpu
from jax.sharding import PartitionSpec as P

SUB = 8
LANES = 128
BLOCKS = 16
FOLD = 2 * BLOCKS
KEPT = BLOCKS + 1
FULL = FOLD * LANES
SIGNAL = 5


def turn(value, step, modulus):
    re, im = value
    step %= modulus
    if step == 0:
        return value
    if 2 * step == modulus:
        return (-re, -im)
    if 4 * step == modulus:
        return (-im, re)
    if 4 * step == 3 * modulus:
        return (im, -re)
    if 8 * step % modulus == 0:
        root = math.sqrt(0.5)
        odd = 8 * step // modulus
        plus, minus = (re + im) * root, (re - im) * root
        if odd == 1:
            return (minus, plus)
        if odd == 3:
            return (-plus, minus)
        if odd == 5:
            return (-minus, -plus)
        return (plus, -minus)
    angle = 2.0 * math.pi * step / modulus
    c, s = math.cos(angle), math.sin(angle)
    return (re * c - im * s, re * s + im * c)


def add(left, right):
    return (left[0] + right[0], left[1] + right[1])


def sub(left, right):
    return (left[0] - right[0], left[1] - right[1])


def dft(values, sign):
    size = len(values)
    if size == 1:
        return values
    even = dft(values[0::2], sign)
    odd = dft(values[1::2], sign)
    odd = [turn(value, sign * k, size) for k, value in enumerate(odd)]
    return [add(e, o) for e, o in zip(even, odd)] + [sub(e, o) for e, o in zip(even, odd)]


def odd_forward(values):
    size = len(values)
    half = size // 2
    if size == 1:
        return {1: (values[0], None)}
    pairs = [turn((values[a], -values[a + half]), -a, 2 * size) for a in range(half)]
    result = {}
    for r, value in enumerate(dft(pairs, -1)):
        k = 4 * r + 1
        if k <= size:
            result[k] = value
        else:
            result[2 * size - k] = (value[0], -value[1])
    return result


def real_forward(values):
    size = len(values)
    if size == 1:
        return {0: (values[0], None)}
    half = size // 2
    sums = [values[a] + values[a + half] for a in range(half)]
    gaps = [values[a] - values[a + half] for a in range(half)]
    result = {2 * k: value for k, value in real_forward(sums).items()}
    result.update(odd_forward(gaps))
    return result


def padded_forward(values):
    result = {2 * k: value for k, value in real_forward(values).items()}
    result.update(odd_forward(values))
    return [result[k] for k in range(len(values) + 1)]


def odd_inverse(spec, size):
    half = size // 2
    if size == 1:
        return [spec[1][0]]
    inputs = []
    for r in range(half):
        k = 4 * r + 1
        if k <= size:
            inputs.append(spec[k])
        else:
            inputs.append((spec[2 * size - k][0], -spec[2 * size - k][1]))
    turned = [turn(value, a, 2 * size) for a, value in enumerate(dft(inputs, 1))]
    return [value[0] for value in turned] + [-value[1] for value in turned]


def real_inverse(spec, size):
    if size == 1:
        return [spec[0][0]]
    half = size // 2
    even = real_inverse({k // 2: v for k, v in spec.items() if k % 2 == 0}, half)
    odd = odd_inverse({k: v for k, v in spec.items() if k % 2 == 1}, half)
    return [e + o for e, o in zip(even, odd)] + [e - o for e, o in zip(even, odd)]


def padded_inverse(spec):
    half = len(spec) - 1
    even = real_inverse({k // 2: spec[k] for k in range(0, half + 1, 2)}, half)
    odd = odd_inverse({k: spec[k] for k in range(1, half + 1, 2)}, half)
    return [e + o for e, o in zip(even, odd)]


def split(value):
    high = value.astype(jnp.bfloat16)
    low = (value - high.astype(jnp.float32)).astype(jnp.bfloat16)
    return high, low


def tables():
    lane = np.arange(LANES)
    angle = 2.0 * np.pi * (np.outer(lane, lane) % LANES) / LANES
    c, s = np.cos(angle), np.sin(angle)
    forward = np.block([[c, -s], [s, c]])
    inverse = np.block([[c, s], [-s, c]])
    matrices = []
    for matrix in (forward, inverse):
        matrix = matrix.astype(np.float32)
        high = matrix.astype(jnp.bfloat16)
        low = (matrix - high.astype(np.float32)).astype(jnp.bfloat16)
        matrices += [high, low]
    angle = 2.0 * np.pi * np.outer(np.arange(KEPT), lane) / FULL
    scale = np.full((KEPT, 1), 2.0 / FULL)
    scale[0] = scale[-1] = 1.0 / FULL
    rows = [np.cos(angle), -np.sin(angle), np.cos(angle) * scale, np.sin(angle) * scale]
    twist = np.stack(rows, 1)[:, :, None, :]
    twist = np.broadcast_to(twist, (KEPT, 4, SUB, LANES)).astype(np.float32)
    return np.stack(matrices), twist


def product(value, matrix_ref, index):
    high, low = split(value)
    big, small = matrix_ref[index], matrix_ref[index + 1]
    dot = functools.partial(jnp.dot, preferred_element_type=jnp.float32)
    return dot(high, big) + (dot(high, small) + dot(low, big))


def kernel(
    seqs, places,
    up_hbm, sig_hbm, taps_hbm, gain_hbm, matrix_hbm, twist_hbm,
    ig_ref, fg_ref,
    up_buf, sig_buf, taps_buf, ig_buf, fg_buf, mid, up_spec, taps_spec, work, one,
    gain_ref, matrix_ref, twist_ref, up_here, sig_here, taps_here,
    send_sem, recv_sem, table_sem, ready,
):
    row, col = lax.axis_index("dp"), lax.axis_index("ctx")
    group = row * places + col
    peers = seqs * places

    def tile(index):
        return pl.ds(pl.multiple_of(index * SUB, SUB), SUB)

    barrier = pltpu.get_barrier_semaphore()
    chip, core = col // 2, lax.rem(col, 2)
    chips = places // 2
    most = chips // 2

    def signal(semaphore, r, c):
        pl.semaphore_signal(
            semaphore, inc=1, device_id={"dp": r, "ctx": c}, device_id_type=pl.DeviceIdType.MESH
        )

    def along(turn):
        return lax.rem(row + turn, seqs)

    def across(hop, other):
        return lax.rem(chip + hop, chips) * 2 + lax.rem(core + other, 2)

    def tell_column(semaphore):
        for turn in range(1, seqs):
            signal(semaphore, along(turn), col)

    for hop in sorted(range(chips), key=lambda n: abs(most - n)):
        for other in range(2):
            if hop != most and (hop, other) != (0, 0):
                signal(barrier, row, across(hop, other))
    tell_column(barrier)

    ahead = [
        (taps_hbm, taps_here),
        (up_hbm, up_here),
        (sig_hbm, sig_here),
        (gain_hbm, gain_ref),
        (matrix_hbm, matrix_ref),
        (twist_hbm, twist_ref),
    ]
    ahead = [pltpu.make_async_copy(src, dst, table_sem.at[i]) for i, (src, dst) in enumerate(ahead)]
    for copy in ahead:
        copy.start()

    pl.semaphore_wait(barrier, places - 3 + seqs - 1)
    signal(ready.at[0], row, across(chips - 1, 0))
    tell_column(ready.at[1])

    def push(src, dst, kind, r, c):
        pltpu.make_async_remote_copy(
            src_ref=src,
            dst_ref=dst,
            send_sem=send_sem.at[kind],
            recv_sem=recv_sem.at[kind],
            device_id={"dp": r, "ctx": c},
            device_id_type=pl.DeviceIdType.MESH,
        ).start()

    def hop_of(step):
        return most + (step + 1) // 2 * (1 - 2 * lax.rem(step, 2))

    def send(src, dst, kind, *turns, steps=(0, chips), apart=False, own=None):
        def put(turn, hop, other):
            r, c = along(turn) if turn else row, across(hop, other)
            place = kind + turn if apart else kind if own is None else own + 2 * hop + other
            push(src(r, c), dst, place, r, c)

        def body(step, carry):
            for other in range(2):
                for turn in turns:
                    put(turn, hop_of(step), other)
            return carry

        lax.fori_loop(steps[0], min(steps[1], chips - 1), body, 0)
        if steps[1] == chips:
            for turn in turns:
                put(turn, 0, 1)
            for turn in turns:
                if turn:
                    put(turn, 0, 0)

    def stay(src, dst, kind):
        pltpu.make_async_copy(src, dst, recv_sem.at[kind]).start()

    def slab(ref):
        return lambda r, c: ref.at[tile(r * places + c)]

    def send_up(*turns, steps):
        send(slab(up_here), up_buf.at[row, col], 0, *turns, steps=steps)

    def send_taps(steps):
        send(slab(taps_here), taps_buf.at[col], 1, 0, steps=steps)

    def send_sig(*turns):
        send(slab(sig_here), sig_buf.at[row, col], SIGNAL, *turns, apart=True)

    opposite, others = (0, 1), (1, chips)
    ahead[0].wait()
    send_taps(others)
    ahead[1].wait()
    send_up(0, steps=others)
    pl.semaphore_wait(ready.at[0], 1)
    tell_column(ready.at[2])
    send_up(0, steps=opposite)
    send_taps(opposite)
    pl.semaphore_wait(ready.at[1], seqs - 1)
    send_up(3, steps=others)
    pl.semaphore_wait(ready.at[2], seqs - 1)
    send_up(3, 2, 1, steps=opposite)
    send_up(2, 1, steps=others)
    ahead[2].wait()
    send_sig(3, 2)
    send_sig(1, 0)
    stay(slab(taps_here)(row, col), taps_buf.at[col], 1)
    stay(slab(up_here)(row, col), up_buf.at[row, col], 0)
    stay(slab(sig_here)(row, col), sig_buf.at[row, col], SIGNAL)

    def arrived(ref, kind):
        pltpu.make_async_copy(ref, ref, recv_sem.at[kind]).wait()

    def left(ref, kind, count):
        part = ref.at[pl.ds(0, count * SUB)]
        pltpu.make_async_copy(part, part, send_sem.at[kind]).wait()

    def fold(load, store):
        spec = padded_forward([load(a) for a in range(BLOCKS)])
        for k, (re, im) in enumerate(spec):
            c, s = twist_ref[k, 0], twist_ref[k, 1]
            if im is None:
                store(k, re * c, re * s)
            else:
                store(k, re * c - im * s, re * s + im * c)

    def unfold(load):
        spec = []
        for k in range(KEPT):
            re, im = load(k)
            c, s = twist_ref[k, 2], twist_ref[k, 3]
            spec.append((re * c - im * s, re * s + im * c))
        return padded_inverse(spec)

    def fold_all(buf):
        def body(b, carry):
            def store(k, re, im):
                mid[k, b, :, :LANES] = re
                mid[k, b, :, LANES:] = im

            fold(lambda a: buf[b, a], store)
            return carry

        lax.fori_loop(0, seqs, body, 0)

    whole = (KEPT * seqs * SUB, 2 * LANES)
    shaped = (KEPT, seqs, SUB, 2 * LANES)

    for copy in ahead[3:]:
        copy.wait()
    lane = lax.broadcasted_iota(jnp.int32, (SUB, LANES), 1)
    channel = lax.broadcasted_iota(jnp.int32, (SUB, LANES), 0) + col * SUB
    gain = jnp.where(lane == channel, gain_ref[pl.ds(row, 1), :], 0.0)
    gain = jnp.sum(gain, axis=1, keepdims=True)

    arrived(taps_buf, 1)

    def store_taps(k, re, im):
        work[k, :, :LANES] = re
        work[k, :, LANES:] = im

    fold(lambda a: taps_buf[a], store_taps)
    taps_spec[...] = product(work[...].reshape(KEPT * SUB, 2 * LANES), matrix_ref, 0).reshape(
        KEPT, SUB, 2 * LANES
    )

    arrived(up_buf, 0)
    fold_all(up_buf)
    up_spec[...] = product(mid[...].reshape(whole), matrix_ref, 0).reshape(shaped)

    def times_taps(k, carry):
        fr, fi = taps_spec[k, :, :LANES], taps_spec[k, :, LANES:]
        for b in range(seqs):
            ur, ui = up_spec[k, b, :, :LANES], up_spec[k, b, :, LANES:]
            mid[k, b, :, :LANES] = ur * fr + ui * fi
            mid[k, b, :, LANES:] = ui * fr - ur * fi
        return carry

    lax.fori_loop(0, KEPT, times_taps, 0)
    mid[...] = product(mid[...].reshape(whole), matrix_ref, 2).reshape(shaped)

    def unfold_input(b, carry):
        values = unfold(lambda k: (mid[k, b, :, :LANES], mid[k, b, :, LANES:]))
        for a in range(BLOCKS):
            ig_buf[b, a] = values[a] + gain * up_buf[b, a]
        return carry

    lax.fori_loop(0, seqs, unfold_input, 0)

    def send_input(*turns):
        send(lambda r, c: ig_buf.at[r, c], ig_ref.at[tile(group)], 2, *turns)

    stay(ig_buf.at[row, col], ig_ref.at[tile(group)], 2)
    for turn in range(1, seqs):
        left(sig_here, SIGNAL + turn, places)
    left(sig_here, SIGNAL, places - 1)
    send_input(3)
    send_input(2)

    work[...] = jnp.zeros_like(work)

    def times_signal(step, carry):
        turn = seqs - 1 - step
        b = lax.rem(row + seqs - turn, seqs)
        arrived(sig_buf.at[b], SIGNAL + turn)

        def store(k, re, im):
            one[k, :, :LANES] = re
            one[k, :, LANES:] = im

        fold(lambda a: sig_buf[b, a], store)
        spec = product(one[...].reshape(KEPT * SUB, 2 * LANES), matrix_ref, 0)
        for k in range(KEPT):
            sr, si = spec[k * SUB : (k + 1) * SUB, :LANES], spec[k * SUB : (k + 1) * SUB, LANES:]
            ur, ui = up_spec[k, b, :, :LANES], up_spec[k, b, :, LANES:]
            work[k, :, :LANES] += ur * sr + ui * si
            work[k, :, LANES:] += ui * sr - ur * si
        return carry

    lax.fori_loop(0, seqs, times_signal, 0)
    work[...] = product(work[...].reshape(KEPT * SUB, 2 * LANES), matrix_ref, 2).reshape(
        KEPT, SUB, 2 * LANES
    )
    values = unfold(lambda k: (work[k, :, :LANES], work[k, :, LANES:]))
    for a in range(BLOCKS):
        fg_buf[a] = values[a] * (1.0 / math.sqrt(seqs * places * LANES))
    first = SIGNAL + seqs
    send(lambda r, c: fg_buf.at[c], fg_ref.at[tile(group)], 3, 0, own=first)
    pltpu.make_async_copy(fg_buf.at[col], fg_ref.at[tile(group)], recv_sem.at[3]).start()
    send_input(1)
    send_input(0)

    def spread(part):
        for turn in (2, 1, 3):
            push(part, part, 4, along(turn), col)

    def pass_on(hop, other):
        part = fg_ref.at[tile(row * places + across(chips - hop, other))]
        arrived(part, first + 2 * hop + other)
        spread(part)

    def pass_on_both(step, carry):
        for other in range(2):
            pass_on(hop_of(chips - 1 - step), other)
        return carry

    part = fg_ref.at[tile(group)]
    arrived(part, 3)
    spread(part)
    pass_on(0, 1)
    lax.fori_loop(1, chips, pass_on_both, 0)

    left(taps_here, 1, places - 1)
    left(up_here, 0, peers - 1)
    left(ig_ref, 2, peers - 1)
    part = fg_ref.at[tile(0)]
    for shift in range(1, places):
        pltpu.make_async_copy(part, part, send_sem.at[first + shift]).wait()
    left(fg_ref, 4, (seqs - 1) * places)
    arrived(ig_ref, 2)
    arrived(fg_ref.at[pl.ds(0, (seqs - 1) * places * SUB)], 4)


def deliver(ig_part, fg_part, ig_ref, fg_ref, sem):
    copies = [
        pltpu.make_async_copy(ig_part, ig_ref, sem.at[0]),
        pltpu.make_async_copy(fg_part, fg_ref, sem.at[1]),
    ]
    for copy in copies:
        copy.start()
    for copy in copies:
        copy.wait()


def shards(signal, upstream, filter_taps, skip_gain):
    seqs, places = lax.axis_size("dp"), lax.axis_size("ctx")
    channels, length = filter_taps.shape
    assert (channels, length, places) == (SUB * seqs * places, LANES, BLOCKS)
    assert places * SUB == LANES
    matrices, twist = tables()
    rows = (channels, length)
    hbm = pl.BlockSpec(memory_space=pltpu.HBM)
    vmem = pl.BlockSpec(memory_space=pltpu.VMEM)
    spec_shape = (KEPT, seqs, SUB, 2 * LANES)
    results = [pltpu.VMEM(rows, jnp.float32)] * 2
    parts = pl.pallas_call(
        functools.partial(kernel, seqs, places),
        out_shape=results,
        in_specs=[hbm] * 6,
        out_specs=[vmem] * 2,
        scratch_shapes=[
            pltpu.VMEM((seqs, places, SUB, LANES), jnp.float32),
            pltpu.VMEM((seqs, places, SUB, LANES), jnp.float32),
            pltpu.VMEM((places, SUB, LANES), jnp.float32),
            pltpu.VMEM((seqs, places, SUB, LANES), jnp.float32),
            pltpu.VMEM((places, SUB, LANES), jnp.float32),
            pltpu.VMEM(spec_shape, jnp.float32),
            pltpu.VMEM(spec_shape, jnp.float32),
            pltpu.VMEM((KEPT, SUB, 2 * LANES), jnp.float32),
            pltpu.VMEM((KEPT, SUB, 2 * LANES), jnp.float32),
            pltpu.VMEM((KEPT, SUB, 2 * LANES), jnp.float32),
            pltpu.VMEM((seqs, LANES), jnp.float32),
            pltpu.VMEM(matrices.shape, jnp.bfloat16),
            pltpu.VMEM(twist.shape, jnp.float32),
            pltpu.VMEM(rows, jnp.float32),
            pltpu.VMEM(rows, jnp.float32),
            pltpu.VMEM(rows, jnp.float32),
            pltpu.SemaphoreType.DMA((SIGNAL + seqs + places,)),
            pltpu.SemaphoreType.DMA((SIGNAL + seqs + places,)),
            pltpu.SemaphoreType.DMA((6,)),
            pltpu.SemaphoreType.REGULAR((3,)),
        ],
        compiler_params=pltpu.CompilerParams(
            collective_id=0, has_side_effects=True, vmem_limit_bytes=32 * 1024 * 1024
        ),
    )(
        *[
            pltpu.with_memory_space_constraint(value, pltpu.HBM)
            for value in (
                upstream[0],
                signal[0],
                filter_taps,
                skip_gain.reshape(seqs, LANES),
                jnp.asarray(matrices),
                jnp.asarray(twist),
            )
        ]
    )
    input_grad, filter_grad = pl.pallas_call(
        deliver,
        out_shape=[pltpu.HBM(rows, jnp.float32)] * 2,
        in_specs=[vmem] * 2,
        out_specs=[hbm] * 2,
        scratch_shapes=[pltpu.SemaphoreType.DMA((2,))],
    )(*[pltpu.with_memory_space_constraint(part, pltpu.VMEM) for part in parts])
    return (input_grad[None], filter_grad)


def solution(mesh):
    placed = (P("dp", "tp", "ctx"), P("dp", "tp", "ctx"), P("tp", "ctx"), P("tp"))
    return jax.shard_map(
        shards,
        mesh=mesh,
        in_specs=placed,
        out_specs=(P("dp", "tp", "ctx"), P("tp", "ctx")),
        check_vma=False,
    )
```

```python
import functools
import math

import jax
import jax.numpy as jnp
import numpy as np
from jax import lax
from jax.experimental import pallas as pl
from jax.experimental.pallas import tpu as pltpu
from jax.sharding import PartitionSpec as P

SUB = 8
LANES = 128
BLOCKS = 16
FOLD = 2 * BLOCKS
KEPT = BLOCKS + 1
FULL = FOLD * LANES
SIGNAL = 5


def turn(value, step, modulus):
    re, im = value
    step %= modulus
    if step == 0:
        return value
    if 2 * step == modulus:
        return (-re, -im)
    if 4 * step == modulus:
        return (-im, re)
    if 4 * step == 3 * modulus:
        return (im, -re)
    if 8 * step % modulus == 0:
        root = math.sqrt(0.5)
        odd = 8 * step // modulus
        plus, minus = (re + im) * root, (re - im) * root
        if odd == 1:
            return (minus, plus)
        if odd == 3:
            return (-plus, minus)
        if odd == 5:
            return (-minus, -plus)
        return (plus, -minus)
    angle = 2.0 * math.pi * step / modulus
    c, s = math.cos(angle), math.sin(angle)
    return (re * c - im * s, re * s + im * c)


def add(left, right):
    return (left[0] + right[0], left[1] + right[1])


def sub(left, right):
    return (left[0] - right[0], left[1] - right[1])


def dft(values, sign):
    size = len(values)
    if size == 1:
        return values
    even = dft(values[0::2], sign)
    odd = dft(values[1::2], sign)
    odd = [turn(value, sign * k, size) for k, value in enumerate(odd)]
    return [add(e, o) for e, o in zip(even, odd)] + [sub(e, o) for e, o in zip(even, odd)]


def odd_forward(values):
    size = len(values)
    half = size // 2
    if size == 1:
        return {1: (values[0], None)}
    pairs = [turn((values[a], -values[a + half]), -a, 2 * size) for a in range(half)]
    result = {}
    for r, value in enumerate(dft(pairs, -1)):
        k = 4 * r + 1
        if k <= size:
            result[k] = value
        else:
            result[2 * size - k] = (value[0], -value[1])
    return result


def real_forward(values):
    size = len(values)
    if size == 1:
        return {0: (values[0], None)}
    half = size // 2
    sums = [values[a] + values[a + half] for a in range(half)]
    gaps = [values[a] - values[a + half] for a in range(half)]
    result = {2 * k: value for k, value in real_forward(sums).items()}
    result.update(odd_forward(gaps))
    return result


def padded_forward(values):
    result = {2 * k: value for k, value in real_forward(values).items()}
    result.update(odd_forward(values))
    return [result[k] for k in range(len(values) + 1)]


def odd_inverse(spec, size):
    half = size // 2
    if size == 1:
        return [spec[1][0]]
    inputs = []
    for r in range(half):
        k = 4 * r + 1
        if k <= size:
            inputs.append(spec[k])
        else:
            inputs.append((spec[2 * size - k][0], -spec[2 * size - k][1]))
    turned = [turn(value, a, 2 * size) for a, value in enumerate(dft(inputs, 1))]
    return [value[0] for value in turned] + [-value[1] for value in turned]


def real_inverse(spec, size):
    if size == 1:
        return [spec[0][0]]
    half = size // 2
    even = real_inverse({k // 2: v for k, v in spec.items() if k % 2 == 0}, half)
    odd = odd_inverse({k: v for k, v in spec.items() if k % 2 == 1}, half)
    return [e + o for e, o in zip(even, odd)] + [e - o for e, o in zip(even, odd)]


def padded_inverse(spec):
    half = len(spec) - 1
    even = real_inverse({k // 2: spec[k] for k in range(0, half + 1, 2)}, half)
    odd = odd_inverse({k: spec[k] for k in range(1, half + 1, 2)}, half)
    return [e + o for e, o in zip(even, odd)]


def split(value):
    high = value.astype(jnp.bfloat16)
    low = (value - high.astype(jnp.float32)).astype(jnp.bfloat16)
    return high, low


def tables():
    lane = np.arange(LANES)
    angle = 2.0 * np.pi * (np.outer(lane, lane) % LANES) / LANES
    c, s = np.cos(angle), np.sin(angle)
    forward = np.block([[c, -s], [s, c]])
    inverse = np.block([[c, s], [-s, c]])
    matrices = []
    for matrix in (forward, inverse):
        matrix = matrix.astype(np.float32)
        high = matrix.astype(jnp.bfloat16)
        low = (matrix - high.astype(np.float32)).astype(jnp.bfloat16)
        matrices += [high, low]
    angle = 2.0 * np.pi * np.outer(np.arange(KEPT), lane) / FULL
    scale = np.full((KEPT, 1), 2.0 / FULL)
    scale[0] = scale[-1] = 1.0 / FULL
    rows = [np.cos(angle), -np.sin(angle), np.cos(angle) * scale, np.sin(angle) * scale]
    twist = np.stack(rows, 1)[:, :, None, :]
    twist = np.broadcast_to(twist, (KEPT, 4, SUB, LANES)).astype(np.float32)
    return np.stack(matrices), twist


def product(value, matrix_ref, index):
    high, low = split(value)
    big, small = matrix_ref[index], matrix_ref[index + 1]
    dot = functools.partial(jnp.dot, preferred_element_type=jnp.float32)
    return dot(high, big) + (dot(high, small) + dot(low, big))


def kernel(
    seqs, places,
    up_hbm, sig_hbm, taps_hbm, gain_hbm, matrix_hbm, twist_hbm,
    ig_ref, fg_ref,
    up_buf, sig_buf, taps_buf, ig_buf, fg_buf, mid, up_spec, taps_spec, work, one,
    gain_ref, matrix_ref, twist_ref, up_here, sig_here, taps_here,
    send_sem, recv_sem, table_sem, ready,
):
    row, col = lax.axis_index("dp"), lax.axis_index("ctx")
    group = row * places + col
    peers = seqs * places

    def tile(index):
        return pl.ds(pl.multiple_of(index * SUB, SUB), SUB)

    barrier = pltpu.get_barrier_semaphore()
    chip, core = col // 2, lax.rem(col, 2)
    chips = places // 2
    most = chips // 2

    def signal(semaphore, r, c):
        pl.semaphore_signal(
            semaphore, inc=1, device_id={"dp": r, "ctx": c}, device_id_type=pl.DeviceIdType.MESH
        )

    def along(turn):
        return lax.rem(row + turn, seqs)

    def across(hop, other):
        return lax.rem(chip + hop, chips) * 2 + lax.rem(core + other, 2)

    def tell_column(semaphore):
        for turn in range(1, seqs):
            signal(semaphore, along(turn), col)

    for hop in sorted(range(chips), key=lambda n: abs(most - n)):
        for other in range(2):
            if hop != most and (hop, other) != (0, 0):
                signal(barrier, row, across(hop, other))
    tell_column(barrier)

    ahead = [
        (taps_hbm, taps_here),
        (up_hbm, up_here),
        (sig_hbm, sig_here),
        (gain_hbm, gain_ref),
        (matrix_hbm, matrix_ref),
        (twist_hbm, twist_ref),
    ]
    ahead = [pltpu.make_async_copy(src, dst, table_sem.at[i]) for i, (src, dst) in enumerate(ahead)]
    for copy in ahead:
        copy.start()

    pl.semaphore_wait(barrier, places - 3 + seqs - 1)
    signal(ready.at[0], row, across(chips - 1, 0))
    tell_column(ready.at[1])

    def push(src, dst, kind, r, c):
        pltpu.make_async_remote_copy(
            src_ref=src,
            dst_ref=dst,
            send_sem=send_sem.at[kind],
            recv_sem=recv_sem.at[kind],
            device_id={"dp": r, "ctx": c},
            device_id_type=pl.DeviceIdType.MESH,
        ).start()

    def hop_of(step):
        return most + (step + 1) // 2 * (1 - 2 * lax.rem(step, 2))

    def send(src, dst, kind, *turns, steps=(0, chips), apart=False, own=None):
        def put(turn, hop, other):
            r, c = along(turn) if turn else row, across(hop, other)
            place = kind + turn if apart else kind if own is None else own + 2 * hop + other
            push(src(r, c), dst, place, r, c)

        def body(step, carry):
            for other in range(2):
                for turn in turns:
                    put(turn, hop_of(step), other)
            return carry

        lax.fori_loop(steps[0], min(steps[1], chips - 1), body, 0)
        if steps[1] == chips:
            for turn in turns:
                put(turn, 0, 1)
            for turn in turns:
                if turn:
                    put(turn, 0, 0)

    def send_half(half, src, dst, kind, *turns, which=None, apart=False):
        other = lax.rem(core + half, 2)

        def put(turn, hop):
            r, c = along(turn) if turn else row, across(hop, other)
            push(src(r, c), dst, kind + turn if apart else kind, r, c)

        def body(step, carry):
            for turn in turns:
                put(turn, hop_of(step))
            return carry

        if which == "opposite":
            body(0, 0)
            return
        lax.fori_loop(1 if which == "others" else 0, chips - 1, body, 0)
        for turn in turns:
            if turn:
                put(turn, 0)
            else:
                pl.when(other == 1)(lambda: put(0, 0))

    def stay(src, dst, kind):
        pltpu.make_async_copy(src, dst, recv_sem.at[kind]).start()

    def slab(ref):
        return lambda r, c: ref.at[tile(r * places + c)]

    def send_up(half, *turns, which=None):
        send_half(half, slab(up_here), up_buf.at[row, col], 0, *turns, which=which)

    def send_taps(half, which=None):
        send_half(half, slab(taps_here), taps_buf.at[col], 1, 0, which=which)

    def send_sig(half, *turns):
        send_half(half, slab(sig_here), sig_buf.at[row, col], SIGNAL, *turns, apart=True)

    ahead[0].wait()
    ahead[1].wait()
    send_taps(0, "others")
    send_up(0, 0, which="others")
    send_taps(1, "others")
    send_up(1, 0, which="others")
    pl.semaphore_wait(ready.at[0], 1)
    tell_column(ready.at[2])
    for half in range(2):
        send_up(half, 0, which="opposite")
        send_taps(half, "opposite")
    pl.semaphore_wait(ready.at[1], seqs - 1)
    send_up(0, 3, which="others")
    pl.semaphore_wait(ready.at[2], seqs - 1)
    send_up(0, 3, 2, 1, which="opposite")
    send_up(0, 2, 1, which="others")
    ahead[2].wait()
    send_sig(0, 3, 2)
    send_sig(0, 1, 0)
    for turn in (3, 2, 1):
        send_up(1, turn)
    send_sig(1, 3, 2)
    send_sig(1, 1, 0)
    stay(slab(taps_here)(row, col), taps_buf.at[col], 1)
    stay(slab(up_here)(row, col), up_buf.at[row, col], 0)
    stay(slab(sig_here)(row, col), sig_buf.at[row, col], SIGNAL)

    def arrived(ref, kind):
        pltpu.make_async_copy(ref, ref, recv_sem.at[kind]).wait()

    def left(ref, kind, count):
        part = ref.at[pl.ds(0, count * SUB)]
        pltpu.make_async_copy(part, part, send_sem.at[kind]).wait()

    def fold(load, store):
        spec = padded_forward([load(a) for a in range(BLOCKS)])
        for k, (re, im) in enumerate(spec):
            c, s = twist_ref[k, 0], twist_ref[k, 1]
            if im is None:
                store(k, re * c, re * s)
            else:
                store(k, re * c - im * s, re * s + im * c)

    def unfold(load):
        spec = []
        for k in range(KEPT):
            re, im = load(k)
            c, s = twist_ref[k, 2], twist_ref[k, 3]
            spec.append((re * c - im * s, re * s + im * c))
        return padded_inverse(spec)

    def fold_all(buf):
        def body(b, carry):
            def store(k, re, im):
                mid[k, b, :, :LANES] = re
                mid[k, b, :, LANES:] = im

            fold(lambda a: buf[b, a], store)
            return carry

        lax.fori_loop(0, seqs, body, 0)

    whole = (KEPT * seqs * SUB, 2 * LANES)
    shaped = (KEPT, seqs, SUB, 2 * LANES)

    for copy in ahead[3:]:
        copy.wait()
    lane = lax.broadcasted_iota(jnp.int32, (SUB, LANES), 1)
    channel = lax.broadcasted_iota(jnp.int32, (SUB, LANES), 0) + col * SUB
    gain = jnp.where(lane == channel, gain_ref[pl.ds(row, 1), :], 0.0)
    gain = jnp.sum(gain, axis=1, keepdims=True)

    arrived(taps_buf, 1)

    def store_taps(k, re, im):
        work[k, :, :LANES] = re
        work[k, :, LANES:] = im

    fold(lambda a: taps_buf[a], store_taps)
    taps_spec[...] = product(work[...].reshape(KEPT * SUB, 2 * LANES), matrix_ref, 0).reshape(
        KEPT, SUB, 2 * LANES
    )

    arrived(up_buf, 0)
    fold_all(up_buf)
    up_spec[...] = product(mid[...].reshape(whole), matrix_ref, 0).reshape(shaped)

    def times_taps(k, carry):
        fr, fi = taps_spec[k, :, :LANES], taps_spec[k, :, LANES:]
        for b in range(seqs):
            ur, ui = up_spec[k, b, :, :LANES], up_spec[k, b, :, LANES:]
            mid[k, b, :, :LANES] = ur * fr + ui * fi
            mid[k, b, :, LANES:] = ui * fr - ur * fi
        return carry

    lax.fori_loop(0, KEPT, times_taps, 0)
    mid[...] = product(mid[...].reshape(whole), matrix_ref, 2).reshape(shaped)

    def unfold_input(b, carry):
        values = unfold(lambda k: (mid[k, b, :, :LANES], mid[k, b, :, LANES:]))
        for a in range(BLOCKS):
            ig_buf[b, a] = values[a] + gain * up_buf[b, a]
        return carry

    lax.fori_loop(0, seqs, unfold_input, 0)

    def send_input(*turns):
        send(lambda r, c: ig_buf.at[r, c], ig_ref.at[tile(group)], 2, *turns)

    stay(ig_buf.at[row, col], ig_ref.at[tile(group)], 2)

    def early():
        for turn in range(1, seqs):
            left(sig_here, SIGNAL + turn, places)
        left(sig_here, SIGNAL, places - 1)
        send_input(3)
        send_input(2)

    pl.when(core == 1)(early)

    work[...] = jnp.zeros_like(work)

    def times_signal(step, carry):
        turn = seqs - 1 - step
        b = lax.rem(row + seqs - turn, seqs)
        arrived(sig_buf.at[b], SIGNAL + turn)

        def store(k, re, im):
            one[k, :, :LANES] = re
            one[k, :, LANES:] = im

        fold(lambda a: sig_buf[b, a], store)
        spec = product(one[...].reshape(KEPT * SUB, 2 * LANES), matrix_ref, 0)
        for k in range(KEPT):
            sr, si = spec[k * SUB : (k + 1) * SUB, :LANES], spec[k * SUB : (k + 1) * SUB, LANES:]
            ur, ui = up_spec[k, b, :, :LANES], up_spec[k, b, :, LANES:]
            work[k, :, :LANES] += ur * sr + ui * si
            work[k, :, LANES:] += ui * sr - ur * si
        return carry

    lax.fori_loop(0, seqs, times_signal, 0)
    work[...] = product(work[...].reshape(KEPT * SUB, 2 * LANES), matrix_ref, 2).reshape(
        KEPT, SUB, 2 * LANES
    )
    values = unfold(lambda k: (work[k, :, :LANES], work[k, :, LANES:]))
    for a in range(BLOCKS):
        fg_buf[a] = values[a] * (1.0 / math.sqrt(seqs * places * LANES))
    first = SIGNAL + seqs
    send(lambda r, c: fg_buf.at[c], fg_ref.at[tile(group)], 3, 0, own=first)
    pltpu.make_async_copy(fg_buf.at[col], fg_ref.at[tile(group)], recv_sem.at[3]).start()
    pl.when(core == 0)(early)
    send_input(1)
    send_input(0)

    def spread(part):
        for turn in (2, 1, 3):
            push(part, part, 4, along(turn), col)

    def pass_on(hop, other):
        part = fg_ref.at[tile(row * places + across(chips - hop, other))]
        arrived(part, first + 2 * hop + other)
        spread(part)

    def pass_on_half(half):
        other = lax.rem(core + half, 2)
        pl.when(other == 1)(lambda: pass_on(0, other))

        def body(step, carry):
            pass_on(hop_of(chips - 1 - step), other)
            return carry

        lax.fori_loop(1, chips, body, 0)

    part = fg_ref.at[tile(group)]
    arrived(part, 3)
    spread(part)
    pass_on_half(0)
    pass_on_half(1)

    left(taps_here, 1, places - 1)
    left(up_here, 0, peers - 1)
    left(ig_ref, 2, peers - 1)
    part = fg_ref.at[tile(0)]
    for shift in range(1, places):
        pltpu.make_async_copy(part, part, send_sem.at[first + shift]).wait()
    left(fg_ref, 4, (seqs - 1) * places)
    arrived(ig_ref, 2)
    arrived(fg_ref.at[pl.ds(0, (seqs - 1) * places * SUB)], 4)


def deliver(ig_part, fg_part, ig_ref, fg_ref, sem):
    copies = [
        pltpu.make_async_copy(ig_part, ig_ref, sem.at[0]),
        pltpu.make_async_copy(fg_part, fg_ref, sem.at[1]),
    ]
    for copy in copies:
        copy.start()
    for copy in copies:
        copy.wait()


def shards(signal, upstream, filter_taps, skip_gain):
    seqs, places = lax.axis_size("dp"), lax.axis_size("ctx")
    channels, length = filter_taps.shape
    assert (channels, length, places) == (SUB * seqs * places, LANES, BLOCKS)
    assert places * SUB == LANES
    matrices, twist = tables()
    rows = (channels, length)
    hbm = pl.BlockSpec(memory_space=pltpu.HBM)
    vmem = pl.BlockSpec(memory_space=pltpu.VMEM)
    spec_shape = (KEPT, seqs, SUB, 2 * LANES)
    results = [pltpu.VMEM(rows, jnp.float32)] * 2
    parts = pl.pallas_call(
        functools.partial(kernel, seqs, places),
        out_shape=results,
        in_specs=[hbm] * 6,
        out_specs=[vmem] * 2,
        scratch_shapes=[
            pltpu.VMEM((seqs, places, SUB, LANES), jnp.float32),
            pltpu.VMEM((seqs, places, SUB, LANES), jnp.float32),
            pltpu.VMEM((places, SUB, LANES), jnp.float32),
            pltpu.VMEM((seqs, places, SUB, LANES), jnp.float32),
            pltpu.VMEM((places, SUB, LANES), jnp.float32),
            pltpu.VMEM(spec_shape, jnp.float32),
            pltpu.VMEM(spec_shape, jnp.float32),
            pltpu.VMEM((KEPT, SUB, 2 * LANES), jnp.float32),
            pltpu.VMEM((KEPT, SUB, 2 * LANES), jnp.float32),
            pltpu.VMEM((KEPT, SUB, 2 * LANES), jnp.float32),
            pltpu.VMEM((seqs, LANES), jnp.float32),
            pltpu.VMEM(matrices.shape, jnp.bfloat16),
            pltpu.VMEM(twist.shape, jnp.float32),
            pltpu.VMEM(rows, jnp.float32),
            pltpu.VMEM(rows, jnp.float32),
            pltpu.VMEM(rows, jnp.float32),
            pltpu.SemaphoreType.DMA((SIGNAL + seqs + places,)),
            pltpu.SemaphoreType.DMA((SIGNAL + seqs + places,)),
            pltpu.SemaphoreType.DMA((6,)),
            pltpu.SemaphoreType.REGULAR((3,)),
        ],
        compiler_params=pltpu.CompilerParams(
            collective_id=0, has_side_effects=True, vmem_limit_bytes=32 * 1024 * 1024
        ),
    )(
        *[
            pltpu.with_memory_space_constraint(value, pltpu.HBM)
            for value in (
                upstream[0],
                signal[0],
                filter_taps,
                skip_gain.reshape(seqs, LANES),
                jnp.asarray(matrices),
                jnp.asarray(twist),
            )
        ]
    )
    input_grad, filter_grad = pl.pallas_call(
        deliver,
        out_shape=[pltpu.HBM(rows, jnp.float32)] * 2,
        in_specs=[vmem] * 2,
        out_specs=[hbm] * 2,
        scratch_shapes=[pltpu.SemaphoreType.DMA((2,))],
    )(*[pltpu.with_memory_space_constraint(part, pltpu.VMEM) for part in parts])
    return (input_grad[None], filter_grad)


def solution(mesh):
    placed = (P("dp", "tp", "ctx"), P("dp", "tp", "ctx"), P("tp", "ctx"), P("tp"))
    return jax.shard_map(
        shards,
        mesh=mesh,
        in_specs=placed,
        out_specs=(P("dp", "tp", "ctx"), P("tp", "ctx")),
        check_vma=False,
    )
```

```python
import functools
import math

import jax
import jax.numpy as jnp
import numpy as np
from jax import lax
from jax.experimental import pallas as pl
from jax.experimental.pallas import tpu as pltpu
from jax.sharding import PartitionSpec as P

SUB = 8
LANES = 128
BLOCKS = 16
FOLD = 2 * BLOCKS
KEPT = BLOCKS + 1
FULL = FOLD * LANES
SIGNAL = 5


def turn(value, step, modulus):
    re, im = value
    step %= modulus
    if step == 0:
        return value
    if 2 * step == modulus:
        return (-re, -im)
    if 4 * step == modulus:
        return (-im, re)
    if 4 * step == 3 * modulus:
        return (im, -re)
    if 8 * step % modulus == 0:
        root = math.sqrt(0.5)
        odd = 8 * step // modulus
        plus, minus = (re + im) * root, (re - im) * root
        if odd == 1:
            return (minus, plus)
        if odd == 3:
            return (-plus, minus)
        if odd == 5:
            return (-minus, -plus)
        return (plus, -minus)
    angle = 2.0 * math.pi * step / modulus
    c, s = math.cos(angle), math.sin(angle)
    return (re * c - im * s, re * s + im * c)


def add(left, right):
    return (left[0] + right[0], left[1] + right[1])


def sub(left, right):
    return (left[0] - right[0], left[1] - right[1])


def dft(values, sign):
    size = len(values)
    if size == 1:
        return values
    even = dft(values[0::2], sign)
    odd = dft(values[1::2], sign)
    odd = [turn(value, sign * k, size) for k, value in enumerate(odd)]
    return [add(e, o) for e, o in zip(even, odd)] + [sub(e, o) for e, o in zip(even, odd)]


def odd_forward(values):
    size = len(values)
    half = size // 2
    if size == 1:
        return {1: (values[0], None)}
    pairs = [turn((values[a], -values[a + half]), -a, 2 * size) for a in range(half)]
    result = {}
    for r, value in enumerate(dft(pairs, -1)):
        k = 4 * r + 1
        if k <= size:
            result[k] = value
        else:
            result[2 * size - k] = (value[0], -value[1])
    return result


def real_forward(values):
    size = len(values)
    if size == 1:
        return {0: (values[0], None)}
    half = size // 2
    sums = [values[a] + values[a + half] for a in range(half)]
    gaps = [values[a] - values[a + half] for a in range(half)]
    result = {2 * k: value for k, value in real_forward(sums).items()}
    result.update(odd_forward(gaps))
    return result


def padded_forward(values):
    result = {2 * k: value for k, value in real_forward(values).items()}
    result.update(odd_forward(values))
    return [result[k] for k in range(len(values) + 1)]


def odd_inverse(spec, size):
    half = size // 2
    if size == 1:
        return [spec[1][0]]
    inputs = []
    for r in range(half):
        k = 4 * r + 1
        if k <= size:
            inputs.append(spec[k])
        else:
            inputs.append((spec[2 * size - k][0], -spec[2 * size - k][1]))
    turned = [turn(value, a, 2 * size) for a, value in enumerate(dft(inputs, 1))]
    return [value[0] for value in turned] + [-value[1] for value in turned]


def real_inverse(spec, size):
    if size == 1:
        return [spec[0][0]]
    half = size // 2
    even = real_inverse({k // 2: v for k, v in spec.items() if k % 2 == 0}, half)
    odd = odd_inverse({k: v for k, v in spec.items() if k % 2 == 1}, half)
    return [e + o for e, o in zip(even, odd)] + [e - o for e, o in zip(even, odd)]


def padded_inverse(spec):
    half = len(spec) - 1
    even = real_inverse({k // 2: spec[k] for k in range(0, half + 1, 2)}, half)
    odd = odd_inverse({k: spec[k] for k in range(1, half + 1, 2)}, half)
    return [e + o for e, o in zip(even, odd)]


def split(value):
    high = value.astype(jnp.bfloat16)
    low = (value - high.astype(jnp.float32)).astype(jnp.bfloat16)
    return high, low


def tables():
    lane = np.arange(LANES)
    angle = 2.0 * np.pi * (np.outer(lane, lane) % LANES) / LANES
    c, s = np.cos(angle), np.sin(angle)
    forward = np.block([[c, -s], [s, c]])
    inverse = np.block([[c, s], [-s, c]])
    matrices = []
    for matrix in (forward, inverse):
        matrix = matrix.astype(np.float32)
        high = matrix.astype(jnp.bfloat16)
        low = (matrix - high.astype(np.float32)).astype(jnp.bfloat16)
        matrices += [high, low]
    angle = 2.0 * np.pi * np.outer(np.arange(KEPT), lane) / FULL
    scale = np.full((KEPT, 1), 2.0 / FULL)
    scale[0] = scale[-1] = 1.0 / FULL
    rows = [np.cos(angle), -np.sin(angle), np.cos(angle) * scale, np.sin(angle) * scale]
    twist = np.stack(rows, 1)[:, :, None, :]
    twist = np.broadcast_to(twist, (KEPT, 4, SUB, LANES)).astype(np.float32)
    return np.stack(matrices), twist


def product(value, matrix_ref, index):
    high, low = split(value)
    big, small = matrix_ref[index], matrix_ref[index + 1]
    dot = functools.partial(jnp.dot, preferred_element_type=jnp.float32)
    return dot(high, big) + (dot(high, small) + dot(low, big))


def kernel(
    seqs, places,
    up_hbm, sig_hbm, taps_hbm, gain_hbm, matrix_hbm, twist_hbm,
    ig_ref, fg_ref,
    up_buf, sig_buf, taps_buf, ig_buf, fg_buf, mid, up_spec, taps_spec, work, one,
    gain_ref, matrix_ref, twist_ref, up_here, sig_here, taps_here,
    send_sem, recv_sem, table_sem, ready,
):
    row, col = lax.axis_index("dp"), lax.axis_index("ctx")
    group = row * places + col
    peers = seqs * places

    def tile(index):
        return pl.ds(pl.multiple_of(index * SUB, SUB), SUB)

    barrier = pltpu.get_barrier_semaphore()
    chip, core = col // 2, lax.rem(col, 2)
    chips = places // 2
    most = chips // 2

    def signal(semaphore, r, c):
        pl.semaphore_signal(
            semaphore, inc=1, device_id={"dp": r, "ctx": c}, device_id_type=pl.DeviceIdType.MESH
        )

    def along(turn):
        return lax.rem(row + turn, seqs)

    def across(hop, other):
        return lax.rem(chip + hop, chips) * 2 + lax.rem(core + other, 2)

    def tell_column(semaphore):
        for turn in range(1, seqs):
            signal(semaphore, along(turn), col)

    for hop in sorted(range(chips), key=lambda n: abs(most - n)):
        for other in range(2):
            if hop != most and (hop, other) != (0, 0):
                signal(barrier, row, across(hop, other))
    tell_column(barrier)

    ahead = [
        (taps_hbm, taps_here),
        (up_hbm, up_here),
        (sig_hbm, sig_here),
        (gain_hbm, gain_ref),
        (matrix_hbm, matrix_ref),
        (twist_hbm, twist_ref),
    ]
    ahead = [pltpu.make_async_copy(src, dst, table_sem.at[i]) for i, (src, dst) in enumerate(ahead)]
    for copy in ahead:
        copy.start()

    pl.semaphore_wait(barrier, places - 3 + seqs - 1)
    signal(ready.at[0], row, across(chips - 1, 0))
    tell_column(ready.at[1])

    def push(src, dst, kind, r, c):
        pltpu.make_async_remote_copy(
            src_ref=src,
            dst_ref=dst,
            send_sem=send_sem.at[kind],
            recv_sem=recv_sem.at[kind],
            device_id={"dp": r, "ctx": c},
            device_id_type=pl.DeviceIdType.MESH,
        ).start()

    def hop_of(step):
        return most + (step + 1) // 2 * (1 - 2 * lax.rem(step, 2))

    def send(src, dst, kind, *turns, steps=(0, chips), apart=False, own=None):
        def put(turn, hop, other):
            r, c = along(turn) if turn else row, across(hop, other)
            place = kind + turn if apart else kind if own is None else own + 2 * hop + other
            push(src(r, c), dst, place, r, c)

        def body(step, carry):
            for other in range(2):
                for turn in turns:
                    put(turn, hop_of(step), other)
            return carry

        lax.fori_loop(steps[0], min(steps[1], chips - 1), body, 0)
        if steps[1] == chips:
            for turn in turns:
                put(turn, 0, 1)
            for turn in turns:
                if turn:
                    put(turn, 0, 0)

    def send_half(half, src, dst, kind, *turns, which=None, apart=False):
        other = lax.rem(core + half, 2)

        def put(turn, hop):
            r, c = along(turn) if turn else row, across(hop, other)
            push(src(r, c), dst, kind + turn if apart else kind, r, c)

        def body(step, carry):
            for turn in turns:
                put(turn, hop_of(step))
            return carry

        if which == "opposite":
            body(0, 0)
            return
        lax.fori_loop(1 if which == "others" else 0, chips - 1, body, 0)
        for turn in turns:
            if turn:
                put(turn, 0)
            else:
                pl.when(other == 1)(lambda: put(0, 0))

    def stay(src, dst, kind):
        pltpu.make_async_copy(src, dst, recv_sem.at[kind]).start()

    def slab(ref):
        return lambda r, c: ref.at[tile(r * places + c)]

    def send_up(half, *turns, which=None):
        send_half(half, slab(up_here), up_buf.at[row, col], 0, *turns, which=which)

    def send_taps(half, which=None):
        send_half(half, slab(taps_here), taps_buf.at[col], 1, 0, which=which)

    def send_sig(half, *turns, which=None):
        send_half(
            half, slab(sig_here), sig_buf.at[row, col], SIGNAL, *turns, which=which, apart=True
        )

    ahead[1].wait()
    send_up(0, 0, which="others")
    send_up(1, 0, which="others")
    ahead[2].wait()
    send_sig(0, 0, which="others")
    pl.semaphore_wait(ready.at[0], 1)
    tell_column(ready.at[2])
    send_up(0, 0, which="opposite")
    send_up(1, 0, which="opposite")
    send_sig(0, 0, which="opposite")
    pl.semaphore_wait(ready.at[1], seqs - 1)
    send_up(0, 3, which="others")
    pl.semaphore_wait(ready.at[2], seqs - 1)
    send_up(0, 3, 2, 1, which="opposite")
    send_up(0, 2, 1, which="others")
    send_sig(0, 3, 2)
    send_sig(0, 1)
    ahead[0].wait()
    send_taps(0)
    for turn in (3, 2, 1):
        send_up(1, turn)
    send_sig(1, 3, 2)
    send_sig(1, 1, 0)
    send_taps(1)
    stay(slab(taps_here)(row, col), taps_buf.at[col], 1)
    stay(slab(up_here)(row, col), up_buf.at[row, col], 0)
    stay(slab(sig_here)(row, col), sig_buf.at[row, col], SIGNAL)

    def arrived(ref, kind):
        pltpu.make_async_copy(ref, ref, recv_sem.at[kind]).wait()

    def left(ref, kind, count):
        part = ref.at[pl.ds(0, count * SUB)]
        pltpu.make_async_copy(part, part, send_sem.at[kind]).wait()

    def fold(load, store):
        spec = padded_forward([load(a) for a in range(BLOCKS)])
        for k, (re, im) in enumerate(spec):
            c, s = twist_ref[k, 0], twist_ref[k, 1]
            if im is None:
                store(k, re * c, re * s)
            else:
                store(k, re * c - im * s, re * s + im * c)

    def unfold(load):
        spec = []
        for k in range(KEPT):
            re, im = load(k)
            c, s = twist_ref[k, 2], twist_ref[k, 3]
            spec.append((re * c - im * s, re * s + im * c))
        return padded_inverse(spec)

    def fold_all(buf):
        def body(b, carry):
            def store(k, re, im):
                mid[k, b, :, :LANES] = re
                mid[k, b, :, LANES:] = im

            fold(lambda a: buf[b, a], store)
            return carry

        lax.fori_loop(0, seqs, body, 0)

    whole = (KEPT * seqs * SUB, 2 * LANES)
    shaped = (KEPT, seqs, SUB, 2 * LANES)

    for copy in ahead[3:]:
        copy.wait()
    lane = lax.broadcasted_iota(jnp.int32, (SUB, LANES), 1)
    channel = lax.broadcasted_iota(jnp.int32, (SUB, LANES), 0) + col * SUB
    gain = jnp.where(lane == channel, gain_ref[pl.ds(row, 1), :], 0.0)
    gain = jnp.sum(gain, axis=1, keepdims=True)

    arrived(up_buf, 0)
    fold_all(up_buf)
    up_spec[...] = product(mid[...].reshape(whole), matrix_ref, 0).reshape(shaped)

    work[...] = jnp.zeros_like(work)

    def times_signal(step, carry):
        turn = seqs - 1 - step
        b = lax.rem(row + seqs - turn, seqs)
        arrived(sig_buf.at[b], SIGNAL + turn)

        def store(k, re, im):
            one[k, :, :LANES] = re
            one[k, :, LANES:] = im

        fold(lambda a: sig_buf[b, a], store)
        spec = product(one[...].reshape(KEPT * SUB, 2 * LANES), matrix_ref, 0)
        for k in range(KEPT):
            sr, si = spec[k * SUB : (k + 1) * SUB, :LANES], spec[k * SUB : (k + 1) * SUB, LANES:]
            ur, ui = up_spec[k, b, :, :LANES], up_spec[k, b, :, LANES:]
            work[k, :, :LANES] += ur * sr + ui * si
            work[k, :, LANES:] += ui * sr - ur * si
        return carry

    lax.fori_loop(0, seqs, times_signal, 0)
    work[...] = product(work[...].reshape(KEPT * SUB, 2 * LANES), matrix_ref, 2).reshape(
        KEPT, SUB, 2 * LANES
    )
    values = unfold(lambda k: (work[k, :, :LANES], work[k, :, LANES:]))
    for a in range(BLOCKS):
        fg_buf[a] = values[a] * (1.0 / math.sqrt(seqs * places * LANES))
    first = SIGNAL + seqs
    send(lambda r, c: fg_buf.at[c], fg_ref.at[tile(group)], 3, 0, own=first)
    pltpu.make_async_copy(fg_buf.at[col], fg_ref.at[tile(group)], recv_sem.at[3]).start()
    def spread(part):
        for turn in (2, 1, 3):
            push(part, part, 4, along(turn), col)

    def pass_on(hop, other):
        part = fg_ref.at[tile(row * places + across(chips - hop, other))]
        arrived(part, first + 2 * hop + other)
        spread(part)

    def pass_on_half(half):
        other = lax.rem(core + half, 2)
        pl.when(other == 1)(lambda: pass_on(0, other))

        def body(step, carry):
            pass_on(hop_of(chips - 1 - step), other)
            return carry

        lax.fori_loop(1, chips, body, 0)

    part = fg_ref.at[tile(group)]
    arrived(part, 3)
    spread(part)
    pl.when(core == 1)(lambda: pass_on_half(0))

    arrived(taps_buf, 1)

    def store_taps(k, re, im):
        work[k, :, :LANES] = re
        work[k, :, LANES:] = im

    fold(lambda a: taps_buf[a], store_taps)
    taps_spec[...] = product(work[...].reshape(KEPT * SUB, 2 * LANES), matrix_ref, 0).reshape(
        KEPT, SUB, 2 * LANES
    )

    def input_row(step, carry):
        turn = seqs - 1 - step
        b = lax.rem(row + turn, seqs)
        for k in range(KEPT):
            fr, fi = taps_spec[k, :, :LANES], taps_spec[k, :, LANES:]
            ur, ui = up_spec[k, b, :, :LANES], up_spec[k, b, :, LANES:]
            one[k, :, :LANES] = ur * fr + ui * fi
            one[k, :, LANES:] = ui * fr - ur * fi
        one[...] = product(one[...].reshape(KEPT * SUB, 2 * LANES), matrix_ref, 2).reshape(
            KEPT, SUB, 2 * LANES
        )
        values = unfold(lambda k: (one[k, :, :LANES], one[k, :, LANES:]))
        for a in range(BLOCKS):
            ig_buf[b, a] = values[a] + gain * up_buf[b, a]

        def put(hop, other):
            c = across(hop, other)
            push(ig_buf.at[b, c], ig_ref.at[tile(group)], 2, b, c)

        def body(step, carry):
            for other in range(2):
                put(hop_of(step), other)
            return carry

        lax.fori_loop(0, chips - 1, body, 0)
        put(0, 1)
        pl.when(turn > 0)(lambda: put(0, 0))
        return carry

    lax.fori_loop(0, seqs, input_row, 0)
    stay(ig_buf.at[row, col], ig_ref.at[tile(group)], 2)

    pl.when(core == 0)(lambda: pass_on_half(0))
    pass_on_half(1)

    for turn in range(1, seqs):
        left(sig_here, SIGNAL + turn, places)
    left(sig_here, SIGNAL, places - 1)
    left(taps_here, 1, places - 1)
    left(up_here, 0, peers - 1)
    left(ig_ref, 2, peers - 1)
    part = fg_ref.at[tile(0)]
    for shift in range(1, places):
        pltpu.make_async_copy(part, part, send_sem.at[first + shift]).wait()
    left(fg_ref, 4, (seqs - 1) * places)
    arrived(ig_ref, 2)
    arrived(fg_ref.at[pl.ds(0, (seqs - 1) * places * SUB)], 4)


def deliver(ig_part, fg_part, ig_ref, fg_ref, sem):
    copies = [
        pltpu.make_async_copy(ig_part, ig_ref, sem.at[0]),
        pltpu.make_async_copy(fg_part, fg_ref, sem.at[1]),
    ]
    for copy in copies:
        copy.start()
    for copy in copies:
        copy.wait()


def shards(signal, upstream, filter_taps, skip_gain):
    seqs, places = lax.axis_size("dp"), lax.axis_size("ctx")
    channels, length = filter_taps.shape
    assert (channels, length, places) == (SUB * seqs * places, LANES, BLOCKS)
    assert places * SUB == LANES
    matrices, twist = tables()
    rows = (channels, length)
    hbm = pl.BlockSpec(memory_space=pltpu.HBM)
    vmem = pl.BlockSpec(memory_space=pltpu.VMEM)
    spec_shape = (KEPT, seqs, SUB, 2 * LANES)
    results = [pltpu.VMEM(rows, jnp.float32)] * 2
    parts = pl.pallas_call(
        functools.partial(kernel, seqs, places),
        out_shape=results,
        in_specs=[hbm] * 6,
        out_specs=[vmem] * 2,
        scratch_shapes=[
            pltpu.VMEM((seqs, places, SUB, LANES), jnp.float32),
            pltpu.VMEM((seqs, places, SUB, LANES), jnp.float32),
            pltpu.VMEM((places, SUB, LANES), jnp.float32),
            pltpu.VMEM((seqs, places, SUB, LANES), jnp.float32),
            pltpu.VMEM((places, SUB, LANES), jnp.float32),
            pltpu.VMEM(spec_shape, jnp.float32),
            pltpu.VMEM(spec_shape, jnp.float32),
            pltpu.VMEM((KEPT, SUB, 2 * LANES), jnp.float32),
            pltpu.VMEM((KEPT, SUB, 2 * LANES), jnp.float32),
            pltpu.VMEM((KEPT, SUB, 2 * LANES), jnp.float32),
            pltpu.VMEM((seqs, LANES), jnp.float32),
            pltpu.VMEM(matrices.shape, jnp.bfloat16),
            pltpu.VMEM(twist.shape, jnp.float32),
            pltpu.VMEM(rows, jnp.float32),
            pltpu.VMEM(rows, jnp.float32),
            pltpu.VMEM(rows, jnp.float32),
            pltpu.SemaphoreType.DMA((SIGNAL + seqs + places,)),
            pltpu.SemaphoreType.DMA((SIGNAL + seqs + places,)),
            pltpu.SemaphoreType.DMA((6,)),
            pltpu.SemaphoreType.REGULAR((3,)),
        ],
        compiler_params=pltpu.CompilerParams(
            collective_id=0, has_side_effects=True, vmem_limit_bytes=32 * 1024 * 1024
        ),
    )(
        *[
            pltpu.with_memory_space_constraint(value, pltpu.HBM)
            for value in (
                upstream[0],
                signal[0],
                filter_taps,
                skip_gain.reshape(seqs, LANES),
                jnp.asarray(matrices),
                jnp.asarray(twist),
            )
        ]
    )
    input_grad, filter_grad = pl.pallas_call(
        deliver,
        out_shape=[pltpu.HBM(rows, jnp.float32)] * 2,
        in_specs=[vmem] * 2,
        out_specs=[hbm] * 2,
        scratch_shapes=[pltpu.SemaphoreType.DMA((2,))],
    )(*[pltpu.with_memory_space_constraint(part, pltpu.VMEM) for part in parts])
    return (input_grad[None], filter_grad)


def solution(mesh):
    placed = (P("dp", "tp", "ctx"), P("dp", "tp", "ctx"), P("tp", "ctx"), P("tp"))
    return jax.shard_map(
        shards,
        mesh=mesh,
        in_specs=placed,
        out_specs=(P("dp", "tp", "ctx"), P("tp", "ctx")),
        check_vma=False,
    )
```

```python
import functools
import math

import jax
import jax.numpy as jnp
import numpy as np
from jax import lax
from jax.experimental import pallas as pl
from jax.experimental.pallas import tpu as pltpu
from jax.sharding import PartitionSpec as P

SUB = 8
LANES = 128
BLOCKS = 16
FOLD = 2 * BLOCKS
KEPT = BLOCKS + 1
FULL = FOLD * LANES
SIGNAL = 5


def turn(value, step, modulus):
    re, im = value
    step %= modulus
    if step == 0:
        return value
    if 2 * step == modulus:
        return (-re, -im)
    if 4 * step == modulus:
        return (-im, re)
    if 4 * step == 3 * modulus:
        return (im, -re)
    if 8 * step % modulus == 0:
        root = math.sqrt(0.5)
        odd = 8 * step // modulus
        plus, minus = (re + im) * root, (re - im) * root
        if odd == 1:
            return (minus, plus)
        if odd == 3:
            return (-plus, minus)
        if odd == 5:
            return (-minus, -plus)
        return (plus, -minus)
    angle = 2.0 * math.pi * step / modulus
    c, s = math.cos(angle), math.sin(angle)
    return (re * c - im * s, re * s + im * c)


def add(left, right):
    return (left[0] + right[0], left[1] + right[1])


def sub(left, right):
    return (left[0] - right[0], left[1] - right[1])


def dft(values, sign):
    size = len(values)
    if size == 1:
        return values
    even = dft(values[0::2], sign)
    odd = dft(values[1::2], sign)
    odd = [turn(value, sign * k, size) for k, value in enumerate(odd)]
    return [add(e, o) for e, o in zip(even, odd)] + [sub(e, o) for e, o in zip(even, odd)]


def odd_forward(values):
    size = len(values)
    half = size // 2
    if size == 1:
        return {1: (values[0], None)}
    pairs = [turn((values[a], -values[a + half]), -a, 2 * size) for a in range(half)]
    result = {}
    for r, value in enumerate(dft(pairs, -1)):
        k = 4 * r + 1
        if k <= size:
            result[k] = value
        else:
            result[2 * size - k] = (value[0], -value[1])
    return result


def real_forward(values):
    size = len(values)
    if size == 1:
        return {0: (values[0], None)}
    half = size // 2
    sums = [values[a] + values[a + half] for a in range(half)]
    gaps = [values[a] - values[a + half] for a in range(half)]
    result = {2 * k: value for k, value in real_forward(sums).items()}
    result.update(odd_forward(gaps))
    return result


def padded_forward(values):
    result = {2 * k: value for k, value in real_forward(values).items()}
    result.update(odd_forward(values))
    return [result[k] for k in range(len(values) + 1)]


def odd_inverse(spec, size):
    half = size // 2
    if size == 1:
        return [spec[1][0]]
    inputs = []
    for r in range(half):
        k = 4 * r + 1
        if k <= size:
            inputs.append(spec[k])
        else:
            inputs.append((spec[2 * size - k][0], -spec[2 * size - k][1]))
    turned = [turn(value, a, 2 * size) for a, value in enumerate(dft(inputs, 1))]
    return [value[0] for value in turned] + [-value[1] for value in turned]


def real_inverse(spec, size):
    if size == 1:
        return [spec[0][0]]
    half = size // 2
    even = real_inverse({k // 2: v for k, v in spec.items() if k % 2 == 0}, half)
    odd = odd_inverse({k: v for k, v in spec.items() if k % 2 == 1}, half)
    return [e + o for e, o in zip(even, odd)] + [e - o for e, o in zip(even, odd)]


def padded_inverse(spec):
    half = len(spec) - 1
    even = real_inverse({k // 2: spec[k] for k in range(0, half + 1, 2)}, half)
    odd = odd_inverse({k: spec[k] for k in range(1, half + 1, 2)}, half)
    return [e + o for e, o in zip(even, odd)]


def split(value):
    high = value.astype(jnp.bfloat16)
    low = (value - high.astype(jnp.float32)).astype(jnp.bfloat16)
    return high, low


def tables():
    lane = np.arange(LANES)
    angle = 2.0 * np.pi * (np.outer(lane, lane) % LANES) / LANES
    c, s = np.cos(angle), np.sin(angle)
    forward = np.block([[c, -s], [s, c]])
    inverse = np.block([[c, s], [-s, c]])
    matrices = []
    for matrix in (forward, inverse):
        matrix = matrix.astype(np.float32)
        high = matrix.astype(jnp.bfloat16)
        low = (matrix - high.astype(np.float32)).astype(jnp.bfloat16)
        matrices += [high, low]
    angle = 2.0 * np.pi * np.outer(np.arange(KEPT), lane) / FULL
    scale = np.full((KEPT, 1), 2.0 / FULL)
    scale[0] = scale[-1] = 1.0 / FULL
    rows = [np.cos(angle), -np.sin(angle), np.cos(angle) * scale, np.sin(angle) * scale]
    twist = np.stack(rows, 1)[:, :, None, :]
    twist = np.broadcast_to(twist, (KEPT, 4, SUB, LANES)).astype(np.float32)
    return np.stack(matrices), twist


def product(value, matrix_ref, index):
    high, low = split(value)
    big, small = matrix_ref[index], matrix_ref[index + 1]
    dot = functools.partial(jnp.dot, preferred_element_type=jnp.float32)
    return dot(high, big) + (dot(high, small) + dot(low, big))


def kernel(
    seqs, places,
    up_hbm, sig_hbm, taps_hbm, gain_hbm, matrix_hbm, twist_hbm,
    ig_ref, fg_ref,
    up_buf, sig_buf, taps_buf, ig_buf, fg_buf, mid, up_spec, taps_spec, work, one,
    gain_ref, matrix_ref, twist_ref, up_here, sig_here, taps_here,
    send_sem, recv_sem, table_sem, ready,
):
    row, col = lax.axis_index("dp"), lax.axis_index("ctx")
    group = row * places + col
    peers = seqs * places

    def tile(index):
        return pl.ds(pl.multiple_of(index * SUB, SUB), SUB)

    barrier = pltpu.get_barrier_semaphore()
    chip, core = col // 2, lax.rem(col, 2)
    chips = places // 2
    most = chips // 2

    def signal(semaphore, r, c):
        pl.semaphore_signal(
            semaphore, inc=1, device_id={"dp": r, "ctx": c}, device_id_type=pl.DeviceIdType.MESH
        )

    def along(turn):
        return lax.rem(row + turn, seqs)

    def across(hop, other):
        return lax.rem(chip + hop, chips) * 2 + lax.rem(core + other, 2)

    def tell_column(semaphore):
        for turn in range(1, seqs):
            signal(semaphore, along(turn), col)

    for hop in sorted(range(chips), key=lambda n: abs(most - n)):
        for other in range(2):
            if hop != most and (hop, other) != (0, 0):
                signal(barrier, row, across(hop, other))
    tell_column(barrier)

    ahead = [
        (taps_hbm, taps_here),
        (up_hbm, up_here),
        (sig_hbm, sig_here),
        (gain_hbm, gain_ref),
        (matrix_hbm, matrix_ref),
        (twist_hbm, twist_ref),
    ]
    ahead = [pltpu.make_async_copy(src, dst, table_sem.at[i]) for i, (src, dst) in enumerate(ahead)]
    for copy in ahead:
        copy.start()

    pl.semaphore_wait(barrier, places - 3 + seqs - 1)
    signal(ready.at[0], row, across(chips - 1, 0))
    tell_column(ready.at[1])

    def push(src, dst, kind, r, c):
        pltpu.make_async_remote_copy(
            src_ref=src,
            dst_ref=dst,
            send_sem=send_sem.at[kind],
            recv_sem=recv_sem.at[kind],
            device_id={"dp": r, "ctx": c},
            device_id_type=pl.DeviceIdType.MESH,
        ).start()

    def hop_of(step):
        return most + (step + 1) // 2 * (1 - 2 * lax.rem(step, 2))

    def send(src, dst, kind, *turns, steps=(0, chips), apart=False, own=None):
        def put(turn, hop, other):
            r, c = along(turn) if turn else row, across(hop, other)
            place = kind + turn if apart else kind if own is None else own + 2 * hop + other
            push(src(r, c), dst, place, r, c)

        def body(step, carry):
            for other in range(2):
                for turn in turns:
                    put(turn, hop_of(step), other)
            return carry

        lax.fori_loop(steps[0], min(steps[1], chips - 1), body, 0)
        if steps[1] == chips:
            for turn in turns:
                put(turn, 0, 1)
            for turn in turns:
                if turn:
                    put(turn, 0, 0)

    def send_half(half, src, dst, kind, *turns, which=None, apart=False):
        other = lax.rem(core + half, 2)

        def put(turn, hop):
            r, c = along(turn) if turn else row, across(hop, other)
            push(src(r, c), dst, kind + turn if apart else kind, r, c)

        def body(step, carry):
            for turn in turns:
                put(turn, hop_of(step))
            return carry

        if which == "opposite":
            body(0, 0)
            return
        lax.fori_loop(1 if which == "others" else 0, chips - 1, body, 0)
        for turn in turns:
            if turn:
                put(turn, 0)
            else:
                pl.when(other == 1)(lambda: put(0, 0))

    def stay(src, dst, kind):
        pltpu.make_async_copy(src, dst, recv_sem.at[kind]).start()

    def slab(ref):
        return lambda r, c: ref.at[tile(r * places + c)]

    def send_up(half, *turns, which=None):
        send_half(half, slab(up_here), up_buf.at[row, col], 0, *turns, which=which)

    def send_taps(half, which=None):
        send_half(half, slab(taps_here), taps_buf.at[col], 1, 0, which=which)

    def send_sig(half, *turns, which=None):
        send_half(
            half, slab(sig_here), sig_buf.at[row, col], SIGNAL, *turns, which=which, apart=True
        )

    ahead[1].wait()
    send_up(0, 0, which="others")
    send_up(1, 0, which="others")
    ahead[2].wait()
    send_sig(0, 0, which="others")
    pl.semaphore_wait(ready.at[0], 1)
    tell_column(ready.at[2])
    send_up(0, 0, which="opposite")
    send_up(1, 0, which="opposite")
    send_sig(0, 0, which="opposite")
    pl.semaphore_wait(ready.at[1], seqs - 1)
    send_up(0, 3, which="others")
    pl.semaphore_wait(ready.at[2], seqs - 1)
    send_up(0, 3, 2, 1, which="opposite")
    send_up(0, 2, 1, which="others")
    send_sig(0, 3, 2)
    send_sig(0, 1)
    ahead[0].wait()
    send_taps(0)
    for turn in (3, 2, 1):
        send_up(1, turn)
    send_sig(1, 3, 2)
    send_sig(1, 1, 0)
    send_taps(1)
    stay(slab(taps_here)(row, col), taps_buf.at[col], 1)
    stay(slab(up_here)(row, col), up_buf.at[row, col], 0)
    stay(slab(sig_here)(row, col), sig_buf.at[row, col], SIGNAL)

    def arrived(ref, kind):
        pltpu.make_async_copy(ref, ref, recv_sem.at[kind]).wait()

    def left(ref, kind, count):
        part = ref.at[pl.ds(0, count * SUB)]
        pltpu.make_async_copy(part, part, send_sem.at[kind]).wait()

    def fold(load, store):
        spec = padded_forward([load(a) for a in range(BLOCKS)])
        for k, (re, im) in enumerate(spec):
            c, s = twist_ref[k, 0], twist_ref[k, 1]
            if im is None:
                store(k, re * c, re * s)
            else:
                store(k, re * c - im * s, re * s + im * c)

    def unfold(load):
        spec = []
        for k in range(KEPT):
            re, im = load(k)
            c, s = twist_ref[k, 2], twist_ref[k, 3]
            spec.append((re * c - im * s, re * s + im * c))
        return padded_inverse(spec)

    def fold_all(buf):
        def body(b, carry):
            def store(k, re, im):
                mid[k, b, :, :LANES] = re
                mid[k, b, :, LANES:] = im

            fold(lambda a: buf[b, a], store)
            return carry

        lax.fori_loop(0, seqs, body, 0)

    whole = (KEPT * seqs * SUB, 2 * LANES)
    shaped = (KEPT, seqs, SUB, 2 * LANES)

    for copy in ahead[3:]:
        copy.wait()
    lane = lax.broadcasted_iota(jnp.int32, (SUB, LANES), 1)
    channel = lax.broadcasted_iota(jnp.int32, (SUB, LANES), 0) + col * SUB
    gain = jnp.where(lane == channel, gain_ref[pl.ds(row, 1), :], 0.0)
    gain = jnp.sum(gain, axis=1, keepdims=True)

    arrived(up_buf, 0)
    fold_all(up_buf)
    up_spec[...] = product(mid[...].reshape(whole), matrix_ref, 0).reshape(shaped)

    work[...] = jnp.zeros_like(work)

    def times_signal(step, carry):
        turn = seqs - 1 - step
        b = lax.rem(row + seqs - turn, seqs)
        arrived(sig_buf.at[b], SIGNAL + turn)

        def store(k, re, im):
            one[k, :, :LANES] = re
            one[k, :, LANES:] = im

        fold(lambda a: sig_buf[b, a], store)
        spec = product(one[...].reshape(KEPT * SUB, 2 * LANES), matrix_ref, 0)
        for k in range(KEPT):
            sr, si = spec[k * SUB : (k + 1) * SUB, :LANES], spec[k * SUB : (k + 1) * SUB, LANES:]
            ur, ui = up_spec[k, b, :, :LANES], up_spec[k, b, :, LANES:]
            work[k, :, :LANES] += ur * sr + ui * si
            work[k, :, LANES:] += ui * sr - ur * si
        return carry

    lax.fori_loop(0, seqs, times_signal, 0)
    work[...] = product(work[...].reshape(KEPT * SUB, 2 * LANES), matrix_ref, 2).reshape(
        KEPT, SUB, 2 * LANES
    )
    values = unfold(lambda k: (work[k, :, :LANES], work[k, :, LANES:]))
    for a in range(BLOCKS):
        fg_buf[a] = values[a] * (1.0 / math.sqrt(seqs * places * LANES))
    first = SIGNAL + seqs
    send(lambda r, c: fg_buf.at[c], fg_ref.at[tile(group)], 3, 0, own=first)
    pltpu.make_async_copy(fg_buf.at[col], fg_ref.at[tile(group)], recv_sem.at[3]).start()
    def spread(part):
        for turn in (2, 1, 3):
            push(part, part, 4, along(turn), col)

    def pass_on(hop, other):
        part = fg_ref.at[tile(row * places + across(chips - hop, other))]
        arrived(part, first + 2 * hop + other)
        spread(part)

    def pass_on_half(half):
        other = lax.rem(core + half, 2)
        pl.when(other == 1)(lambda: pass_on(0, other))

        def body(step, carry):
            pass_on(hop_of(chips - 1 - step), other)
            return carry

        lax.fori_loop(1, chips, body, 0)

    part = fg_ref.at[tile(group)]
    arrived(part, 3)
    spread(part)

    arrived(taps_buf, 1)

    def store_taps(k, re, im):
        work[k, :, :LANES] = re
        work[k, :, LANES:] = im

    fold(lambda a: taps_buf[a], store_taps)
    taps_spec[...] = product(work[...].reshape(KEPT * SUB, 2 * LANES), matrix_ref, 0).reshape(
        KEPT, SUB, 2 * LANES
    )

    def input_row(step, carry):
        turn = seqs - 1 - step
        b = lax.rem(row + turn, seqs)
        for k in range(KEPT):
            fr, fi = taps_spec[k, :, :LANES], taps_spec[k, :, LANES:]
            ur, ui = up_spec[k, b, :, :LANES], up_spec[k, b, :, LANES:]
            one[k, :, :LANES] = ur * fr + ui * fi
            one[k, :, LANES:] = ui * fr - ur * fi
        one[...] = product(one[...].reshape(KEPT * SUB, 2 * LANES), matrix_ref, 2).reshape(
            KEPT, SUB, 2 * LANES
        )
        values = unfold(lambda k: (one[k, :, :LANES], one[k, :, LANES:]))
        for a in range(BLOCKS):
            ig_buf[b, a] = values[a] + gain * up_buf[b, a]

        def put(hop, other):
            c = across(hop, other)
            push(ig_buf.at[b, c], ig_ref.at[tile(group)], 2, b, c)

        def body(step, carry):
            for other in range(2):
                put(hop_of(step), other)
            return carry

        lax.fori_loop(0, chips - 1, body, 0)
        put(0, 1)
        pl.when(turn > 0)(lambda: put(0, 0))
        return carry

    lax.fori_loop(0, 1, input_row, 0)
    pl.when(core == 1)(lambda: pass_on_half(0))
    lax.fori_loop(1, seqs, input_row, 0)
    stay(ig_buf.at[row, col], ig_ref.at[tile(group)], 2)

    pl.when(core == 0)(lambda: pass_on_half(0))
    pass_on_half(1)

    for turn in range(1, seqs):
        left(sig_here, SIGNAL + turn, places)
    left(sig_here, SIGNAL, places - 1)
    left(taps_here, 1, places - 1)
    left(up_here, 0, peers - 1)
    left(ig_ref, 2, peers - 1)
    part = fg_ref.at[tile(0)]
    for shift in range(1, places):
        pltpu.make_async_copy(part, part, send_sem.at[first + shift]).wait()
    left(fg_ref, 4, (seqs - 1) * places)
    arrived(ig_ref, 2)
    arrived(fg_ref.at[pl.ds(0, (seqs - 1) * places * SUB)], 4)


def deliver(ig_part, fg_part, ig_ref, fg_ref, sem):
    copies = [
        pltpu.make_async_copy(ig_part, ig_ref, sem.at[0]),
        pltpu.make_async_copy(fg_part, fg_ref, sem.at[1]),
    ]
    for copy in copies:
        copy.start()
    for copy in copies:
        copy.wait()


def shards(signal, upstream, filter_taps, skip_gain):
    seqs, places = lax.axis_size("dp"), lax.axis_size("ctx")
    channels, length = filter_taps.shape
    assert (channels, length, places) == (SUB * seqs * places, LANES, BLOCKS)
    assert places * SUB == LANES
    matrices, twist = tables()
    rows = (channels, length)
    hbm = pl.BlockSpec(memory_space=pltpu.HBM)
    vmem = pl.BlockSpec(memory_space=pltpu.VMEM)
    spec_shape = (KEPT, seqs, SUB, 2 * LANES)
    results = [pltpu.VMEM(rows, jnp.float32)] * 2
    parts = pl.pallas_call(
        functools.partial(kernel, seqs, places),
        out_shape=results,
        in_specs=[hbm] * 6,
        out_specs=[vmem] * 2,
        scratch_shapes=[
            pltpu.VMEM((seqs, places, SUB, LANES), jnp.float32),
            pltpu.VMEM((seqs, places, SUB, LANES), jnp.float32),
            pltpu.VMEM((places, SUB, LANES), jnp.float32),
            pltpu.VMEM((seqs, places, SUB, LANES), jnp.float32),
            pltpu.VMEM((places, SUB, LANES), jnp.float32),
            pltpu.VMEM(spec_shape, jnp.float32),
            pltpu.VMEM(spec_shape, jnp.float32),
            pltpu.VMEM((KEPT, SUB, 2 * LANES), jnp.float32),
            pltpu.VMEM((KEPT, SUB, 2 * LANES), jnp.float32),
            pltpu.VMEM((KEPT, SUB, 2 * LANES), jnp.float32),
            pltpu.VMEM((seqs, LANES), jnp.float32),
            pltpu.VMEM(matrices.shape, jnp.bfloat16),
            pltpu.VMEM(twist.shape, jnp.float32),
            pltpu.VMEM(rows, jnp.float32),
            pltpu.VMEM(rows, jnp.float32),
            pltpu.VMEM(rows, jnp.float32),
            pltpu.SemaphoreType.DMA((SIGNAL + seqs + places,)),
            pltpu.SemaphoreType.DMA((SIGNAL + seqs + places,)),
            pltpu.SemaphoreType.DMA((6,)),
            pltpu.SemaphoreType.REGULAR((3,)),
        ],
        compiler_params=pltpu.CompilerParams(
            collective_id=0, has_side_effects=True, vmem_limit_bytes=32 * 1024 * 1024
        ),
    )(
        *[
            pltpu.with_memory_space_constraint(value, pltpu.HBM)
            for value in (
                upstream[0],
                signal[0],
                filter_taps,
                skip_gain.reshape(seqs, LANES),
                jnp.asarray(matrices),
                jnp.asarray(twist),
            )
        ]
    )
    input_grad, filter_grad = pl.pallas_call(
        deliver,
        out_shape=[pltpu.HBM(rows, jnp.float32)] * 2,
        in_specs=[vmem] * 2,
        out_specs=[hbm] * 2,
        scratch_shapes=[pltpu.SemaphoreType.DMA((2,))],
    )(*[pltpu.with_memory_space_constraint(part, pltpu.VMEM) for part in parts])
    return (input_grad[None], filter_grad)


def solution(mesh):
    placed = (P("dp", "tp", "ctx"), P("dp", "tp", "ctx"), P("tp", "ctx"), P("tp"))
    return jax.shard_map(
        shards,
        mesh=mesh,
        in_specs=placed,
        out_specs=(P("dp", "tp", "ctx"), P("tp", "ctx")),
        check_vma=False,
    )
```

```python
import functools
import math

import jax
import jax.numpy as jnp
import numpy as np
from jax import lax
from jax.experimental import pallas as pl
from jax.experimental.pallas import tpu as pltpu
from jax.sharding import PartitionSpec as P

SUB = 8
LANES = 128
BLOCKS = 16
FOLD = 2 * BLOCKS
KEPT = BLOCKS + 1
FULL = FOLD * LANES
SIGNAL = 5


def turn(value, step, modulus):
    re, im = value
    step %= modulus
    if step == 0:
        return value
    if 2 * step == modulus:
        return (-re, -im)
    if 4 * step == modulus:
        return (-im, re)
    if 4 * step == 3 * modulus:
        return (im, -re)
    if 8 * step % modulus == 0:
        root = math.sqrt(0.5)
        odd = 8 * step // modulus
        plus, minus = (re + im) * root, (re - im) * root
        if odd == 1:
            return (minus, plus)
        if odd == 3:
            return (-plus, minus)
        if odd == 5:
            return (-minus, -plus)
        return (plus, -minus)
    angle = 2.0 * math.pi * step / modulus
    c, s = math.cos(angle), math.sin(angle)
    return (re * c - im * s, re * s + im * c)


def add(left, right):
    return (left[0] + right[0], left[1] + right[1])


def sub(left, right):
    return (left[0] - right[0], left[1] - right[1])


def dft(values, sign):
    size = len(values)
    if size == 1:
        return values
    even = dft(values[0::2], sign)
    odd = dft(values[1::2], sign)
    odd = [turn(value, sign * k, size) for k, value in enumerate(odd)]
    return [add(e, o) for e, o in zip(even, odd)] + [sub(e, o) for e, o in zip(even, odd)]


def odd_forward(values):
    size = len(values)
    half = size // 2
    if size == 1:
        return {1: (values[0], None)}
    pairs = [turn((values[a], -values[a + half]), -a, 2 * size) for a in range(half)]
    result = {}
    for r, value in enumerate(dft(pairs, -1)):
        k = 4 * r + 1
        if k <= size:
            result[k] = value
        else:
            result[2 * size - k] = (value[0], -value[1])
    return result


def real_forward(values):
    size = len(values)
    if size == 1:
        return {0: (values[0], None)}
    half = size // 2
    sums = [values[a] + values[a + half] for a in range(half)]
    gaps = [values[a] - values[a + half] for a in range(half)]
    result = {2 * k: value for k, value in real_forward(sums).items()}
    result.update(odd_forward(gaps))
    return result


def padded_forward(values):
    result = {2 * k: value for k, value in real_forward(values).items()}
    result.update(odd_forward(values))
    return [result[k] for k in range(len(values) + 1)]


def odd_inverse(spec, size):
    half = size // 2
    if size == 1:
        return [spec[1][0]]
    inputs = []
    for r in range(half):
        k = 4 * r + 1
        if k <= size:
            inputs.append(spec[k])
        else:
            inputs.append((spec[2 * size - k][0], -spec[2 * size - k][1]))
    turned = [turn(value, a, 2 * size) for a, value in enumerate(dft(inputs, 1))]
    return [value[0] for value in turned] + [-value[1] for value in turned]


def real_inverse(spec, size):
    if size == 1:
        return [spec[0][0]]
    half = size // 2
    even = real_inverse({k // 2: v for k, v in spec.items() if k % 2 == 0}, half)
    odd = odd_inverse({k: v for k, v in spec.items() if k % 2 == 1}, half)
    return [e + o for e, o in zip(even, odd)] + [e - o for e, o in zip(even, odd)]


def padded_inverse(spec):
    half = len(spec) - 1
    even = real_inverse({k // 2: spec[k] for k in range(0, half + 1, 2)}, half)
    odd = odd_inverse({k: spec[k] for k in range(1, half + 1, 2)}, half)
    return [e + o for e, o in zip(even, odd)]


def tables():
    lane = np.arange(LANES)
    angle = 2.0 * np.pi * (np.outer(lane, lane) % LANES) / LANES
    c, s = np.cos(angle), np.sin(angle)
    forward = np.block([[c, -s], [s, c]])
    inverse = np.block([[c, s], [-s, c]])
    matrices = []
    for matrix in (forward, inverse):
        matrix = matrix.astype(np.float32)
        high = matrix.astype(jnp.bfloat16)
        low = (matrix - high.astype(np.float32)).astype(jnp.bfloat16)
        matrices += [high, low]
    angle = 2.0 * np.pi * np.outer(np.arange(KEPT), lane) / FULL
    scale = np.full((KEPT, 1), 2.0 / FULL)
    scale[0] = scale[-1] = 1.0 / FULL
    rows = [np.cos(angle), -np.sin(angle), np.cos(angle) * scale, np.sin(angle) * scale]
    twist = np.stack(rows, 1)[:, :, None, :]
    twist = np.broadcast_to(twist, (KEPT, 4, SUB, LANES)).astype(np.float32)
    return np.stack(matrices), twist


def product(value, matrix_ref, index):
    big, small = matrix_ref[index], matrix_ref[index + 1]
    dot = functools.partial(jnp.dot, preferred_element_type=jnp.float32)
    rows = value.shape[0]
    high = value.astype(jnp.bfloat16)
    exact = high.astype(jnp.float32)
    both = jnp.concatenate([exact, value - exact], axis=0).astype(jnp.bfloat16)
    first = dot(both, big)
    return first[:rows] + (dot(high, small) + first[rows:])


def kernel(
    seqs, places,
    up_hbm, sig_hbm, taps_hbm, gain_hbm, matrix_hbm, twist_hbm,
    ig_ref, fg_ref,
    up_buf, sig_buf, taps_buf, ig_buf, fg_buf, mid, up_spec, taps_spec, work, one,
    gain_ref, matrix_ref, twist_ref, up_here, sig_here, taps_here,
    send_sem, recv_sem, table_sem, ready,
):
    row, col = lax.axis_index("dp"), lax.axis_index("ctx")
    group = row * places + col
    peers = seqs * places

    def tile(index):
        return pl.ds(pl.multiple_of(index * SUB, SUB), SUB)

    barrier = pltpu.get_barrier_semaphore()
    chip, core = col // 2, lax.rem(col, 2)
    chips = places // 2
    most = chips // 2

    def signal(semaphore, r, c):
        pl.semaphore_signal(
            semaphore, inc=1, device_id={"dp": r, "ctx": c}, device_id_type=pl.DeviceIdType.MESH
        )

    def along(turn):
        return lax.rem(row + turn, seqs)

    def across(hop, other):
        return lax.rem(chip + hop, chips) * 2 + lax.rem(core + other, 2)

    def tell_column(semaphore):
        for turn in range(1, seqs):
            signal(semaphore, along(turn), col)

    for hop in sorted(range(chips), key=lambda n: abs(most - n)):
        for other in range(2):
            if hop != most and (hop, other) != (0, 0):
                signal(barrier, row, across(hop, other))
    tell_column(barrier)

    ahead = [
        (taps_hbm, taps_here),
        (up_hbm, up_here),
        (sig_hbm, sig_here),
        (gain_hbm, gain_ref),
        (matrix_hbm, matrix_ref),
        (twist_hbm, twist_ref),
    ]
    ahead = [pltpu.make_async_copy(src, dst, table_sem.at[i]) for i, (src, dst) in enumerate(ahead)]
    for copy in ahead:
        copy.start()

    pl.semaphore_wait(barrier, places - 3 + seqs - 1)
    signal(ready.at[0], row, across(chips - 1, 0))
    tell_column(ready.at[1])

    def push(src, dst, kind, r, c):
        pltpu.make_async_remote_copy(
            src_ref=src,
            dst_ref=dst,
            send_sem=send_sem.at[kind],
            recv_sem=recv_sem.at[kind],
            device_id={"dp": r, "ctx": c},
            device_id_type=pl.DeviceIdType.MESH,
        ).start()

    def hop_of(step):
        return most + (step + 1) // 2 * (1 - 2 * lax.rem(step, 2))

    def send(src, dst, kind, *turns, steps=(0, chips), apart=False, own=None):
        def put(turn, hop, other):
            r, c = along(turn) if turn else row, across(hop, other)
            place = kind + turn if apart else kind if own is None else own + 2 * hop + other
            push(src(r, c), dst, place, r, c)

        def body(step, carry):
            for other in range(2):
                for turn in turns:
                    put(turn, hop_of(step), other)
            return carry

        lax.fori_loop(steps[0], min(steps[1], chips - 1), body, 0)
        if steps[1] == chips:
            for turn in turns:
                put(turn, 0, 1)
            for turn in turns:
                if turn:
                    put(turn, 0, 0)

    def send_half(half, src, dst, kind, *turns, which=None, apart=False):
        other = lax.rem(core + half, 2)

        def put(turn, hop):
            r, c = along(turn) if turn else row, across(hop, other)
            push(src(r, c), dst, kind + turn if apart else kind, r, c)

        def body(step, carry):
            for turn in turns:
                put(turn, hop_of(step))
            return carry

        if which == "opposite":
            body(0, 0)
            return
        lax.fori_loop(1 if which == "others" else 0, chips - 1, body, 0)
        for turn in turns:
            if turn:
                put(turn, 0)
            else:
                pl.when(other == 1)(lambda: put(0, 0))

    def stay(src, dst, kind):
        pltpu.make_async_copy(src, dst, recv_sem.at[kind]).start()

    def slab(ref):
        return lambda r, c: ref.at[tile(r * places + c)]

    def send_up(half, *turns, which=None):
        send_half(half, slab(up_here), up_buf.at[row, col], 0, *turns, which=which)

    def send_taps(half, which=None):
        send_half(half, slab(taps_here), taps_buf.at[col], 1, 0, which=which)

    def send_sig(half, *turns, which=None):
        send_half(
            half, slab(sig_here), sig_buf.at[row, col], SIGNAL, *turns, which=which, apart=True
        )

    ahead[1].wait()
    send_up(0, 0, which="others")
    send_up(1, 0, which="others")
    ahead[2].wait()
    send_sig(0, 0, which="others")
    pl.semaphore_wait(ready.at[0], 1)
    tell_column(ready.at[2])
    send_up(0, 0, which="opposite")
    send_up(1, 0, which="opposite")
    send_sig(0, 0, which="opposite")
    pl.semaphore_wait(ready.at[1], seqs - 1)
    send_up(0, 3, which="others")
    pl.semaphore_wait(ready.at[2], seqs - 1)
    send_up(0, 3, 2, 1, which="opposite")
    send_up(0, 2, 1, which="others")
    send_sig(0, 3, 2)
    send_sig(0, 1)
    ahead[0].wait()
    send_taps(0)
    for turn in (3, 2, 1):
        send_up(1, turn)
    send_sig(1, 3, 2)
    send_sig(1, 1, 0)
    send_taps(1)
    stay(slab(taps_here)(row, col), taps_buf.at[col], 1)
    stay(slab(up_here)(row, col), up_buf.at[row, col], 0)
    stay(slab(sig_here)(row, col), sig_buf.at[row, col], SIGNAL)

    def arrived(ref, kind):
        pltpu.make_async_copy(ref, ref, recv_sem.at[kind]).wait()

    def left(ref, kind, count):
        part = ref.at[pl.ds(0, count * SUB)]
        pltpu.make_async_copy(part, part, send_sem.at[kind]).wait()

    def fold(load, store):
        spec = padded_forward([load(a) for a in range(BLOCKS)])
        for k, (re, im) in enumerate(spec):
            c, s = twist_ref[k, 0], twist_ref[k, 1]
            if im is None:
                store(k, re * c, re * s)
            else:
                store(k, re * c - im * s, re * s + im * c)

    def unfold(load):
        spec = []
        for k in range(KEPT):
            re, im = load(k)
            c, s = twist_ref[k, 2], twist_ref[k, 3]
            spec.append((re * c - im * s, re * s + im * c))
        return padded_inverse(spec)

    def fold_all(buf):
        def body(b, carry):
            def store(k, re, im):
                mid[k, b, :, :LANES] = re
                mid[k, b, :, LANES:] = im

            fold(lambda a: buf[b, a], store)
            return carry

        lax.fori_loop(0, seqs, body, 0)

    whole = (KEPT * seqs * SUB, 2 * LANES)
    shaped = (KEPT, seqs, SUB, 2 * LANES)

    for copy in ahead[3:]:
        copy.wait()
    lane = lax.broadcasted_iota(jnp.int32, (SUB, LANES), 1)
    channel = lax.broadcasted_iota(jnp.int32, (SUB, LANES), 0) + col * SUB
    gain = jnp.where(lane == channel, gain_ref[pl.ds(row, 1), :], 0.0)
    gain = jnp.sum(gain, axis=1, keepdims=True)

    arrived(up_buf, 0)
    fold_all(up_buf)
    up_spec[...] = product(mid[...].reshape(whole), matrix_ref, 0).reshape(shaped)

    work[...] = jnp.zeros_like(work)

    def times_signal(step, carry):
        turn = seqs - 1 - step
        b = lax.rem(row + seqs - turn, seqs)
        arrived(sig_buf.at[b], SIGNAL + turn)

        def store(k, re, im):
            one[k, :, :LANES] = re
            one[k, :, LANES:] = im

        fold(lambda a: sig_buf[b, a], store)
        spec = product(one[...].reshape(KEPT * SUB, 2 * LANES), matrix_ref, 0)
        for k in range(KEPT):
            sr, si = spec[k * SUB : (k + 1) * SUB, :LANES], spec[k * SUB : (k + 1) * SUB, LANES:]
            ur, ui = up_spec[k, b, :, :LANES], up_spec[k, b, :, LANES:]
            work[k, :, :LANES] += ur * sr + ui * si
            work[k, :, LANES:] += ui * sr - ur * si
        return carry

    lax.fori_loop(0, seqs, times_signal, 0)
    work[...] = product(work[...].reshape(KEPT * SUB, 2 * LANES), matrix_ref, 2).reshape(
        KEPT, SUB, 2 * LANES
    )
    values = unfold(lambda k: (work[k, :, :LANES], work[k, :, LANES:]))
    for a in range(BLOCKS):
        fg_buf[a] = values[a] * (1.0 / math.sqrt(seqs * places * LANES))
    first = SIGNAL + seqs
    send(lambda r, c: fg_buf.at[c], fg_ref.at[tile(group)], 3, 0, own=first)
    pltpu.make_async_copy(fg_buf.at[col], fg_ref.at[tile(group)], recv_sem.at[3]).start()
    def spread(part):
        for turn in (2, 1, 3):
            push(part, part, 4, along(turn), col)

    def pass_on(hop, other):
        part = fg_ref.at[tile(row * places + across(chips - hop, other))]
        arrived(part, first + 2 * hop + other)
        spread(part)

    def pass_on_half(half):
        other = lax.rem(core + half, 2)
        pl.when(other == 1)(lambda: pass_on(0, other))

        def body(step, carry):
            pass_on(hop_of(chips - 1 - step), other)
            return carry

        lax.fori_loop(1, chips, body, 0)

    part = fg_ref.at[tile(group)]
    arrived(part, 3)
    spread(part)

    arrived(taps_buf, 1)

    def store_taps(k, re, im):
        work[k, :, :LANES] = re
        work[k, :, LANES:] = im

    fold(lambda a: taps_buf[a], store_taps)
    taps_spec[...] = product(work[...].reshape(KEPT * SUB, 2 * LANES), matrix_ref, 0).reshape(
        KEPT, SUB, 2 * LANES
    )

    def input_row(step, carry):
        turn = seqs - 1 - step
        b = lax.rem(row + turn, seqs)
        for k in range(KEPT):
            fr, fi = taps_spec[k, :, :LANES], taps_spec[k, :, LANES:]
            ur, ui = up_spec[k, b, :, :LANES], up_spec[k, b, :, LANES:]
            one[k, :, :LANES] = ur * fr + ui * fi
            one[k, :, LANES:] = ui * fr - ur * fi
        one[...] = product(one[...].reshape(KEPT * SUB, 2 * LANES), matrix_ref, 2).reshape(
            KEPT, SUB, 2 * LANES
        )
        values = unfold(lambda k: (one[k, :, :LANES], one[k, :, LANES:]))
        for a in range(BLOCKS):
            ig_buf[b, a] = values[a] + gain * up_buf[b, a]

        def put(hop, other):
            c = across(hop, other)
            push(ig_buf.at[b, c], ig_ref.at[tile(group)], 2, b, c)

        def body(step, carry):
            for other in range(2):
                put(hop_of(step), other)
            return carry

        lax.fori_loop(0, chips - 1, body, 0)
        put(0, 1)
        pl.when(turn > 0)(lambda: put(0, 0))
        return carry

    lax.fori_loop(0, 1, input_row, 0)
    pl.when(core == 1)(lambda: pass_on_half(0))
    lax.fori_loop(1, seqs, input_row, 0)
    stay(ig_buf.at[row, col], ig_ref.at[tile(group)], 2)

    pl.when(core == 0)(lambda: pass_on_half(0))
    pass_on_half(1)

    for turn in range(1, seqs):
        left(sig_here, SIGNAL + turn, places)
    left(sig_here, SIGNAL, places - 1)
    left(taps_here, 1, places - 1)
    left(up_here, 0, peers - 1)
    left(ig_ref, 2, peers - 1)
    part = fg_ref.at[tile(0)]
    for shift in range(1, places):
        pltpu.make_async_copy(part, part, send_sem.at[first + shift]).wait()
    left(fg_ref, 4, (seqs - 1) * places)
    arrived(ig_ref, 2)
    arrived(fg_ref.at[pl.ds(0, (seqs - 1) * places * SUB)], 4)


def deliver(ig_part, fg_part, ig_ref, fg_ref, sem):
    copies = [
        pltpu.make_async_copy(ig_part, ig_ref, sem.at[0]),
        pltpu.make_async_copy(fg_part, fg_ref, sem.at[1]),
    ]
    for copy in copies:
        copy.start()
    for copy in copies:
        copy.wait()


def shards(signal, upstream, filter_taps, skip_gain):
    seqs, places = lax.axis_size("dp"), lax.axis_size("ctx")
    channels, length = filter_taps.shape
    assert (channels, length, places) == (SUB * seqs * places, LANES, BLOCKS)
    assert places * SUB == LANES
    matrices, twist = tables()
    rows = (channels, length)
    hbm = pl.BlockSpec(memory_space=pltpu.HBM)
    vmem = pl.BlockSpec(memory_space=pltpu.VMEM)
    spec_shape = (KEPT, seqs, SUB, 2 * LANES)
    results = [pltpu.VMEM(rows, jnp.float32)] * 2
    parts = pl.pallas_call(
        functools.partial(kernel, seqs, places),
        out_shape=results,
        in_specs=[hbm] * 6,
        out_specs=[vmem] * 2,
        scratch_shapes=[
            pltpu.VMEM((seqs, places, SUB, LANES), jnp.float32),
            pltpu.VMEM((seqs, places, SUB, LANES), jnp.float32),
            pltpu.VMEM((places, SUB, LANES), jnp.float32),
            pltpu.VMEM((seqs, places, SUB, LANES), jnp.float32),
            pltpu.VMEM((places, SUB, LANES), jnp.float32),
            pltpu.VMEM(spec_shape, jnp.float32),
            pltpu.VMEM(spec_shape, jnp.float32),
            pltpu.VMEM((KEPT, SUB, 2 * LANES), jnp.float32),
            pltpu.VMEM((KEPT, SUB, 2 * LANES), jnp.float32),
            pltpu.VMEM((KEPT, SUB, 2 * LANES), jnp.float32),
            pltpu.VMEM((seqs, LANES), jnp.float32),
            pltpu.VMEM(matrices.shape, jnp.bfloat16),
            pltpu.VMEM(twist.shape, jnp.float32),
            pltpu.VMEM(rows, jnp.float32),
            pltpu.VMEM(rows, jnp.float32),
            pltpu.VMEM(rows, jnp.float32),
            pltpu.SemaphoreType.DMA((SIGNAL + seqs + places,)),
            pltpu.SemaphoreType.DMA((SIGNAL + seqs + places,)),
            pltpu.SemaphoreType.DMA((6,)),
            pltpu.SemaphoreType.REGULAR((3,)),
        ],
        compiler_params=pltpu.CompilerParams(
            collective_id=0, has_side_effects=True, vmem_limit_bytes=32 * 1024 * 1024
        ),
    )(
        *[
            pltpu.with_memory_space_constraint(value, pltpu.HBM)
            for value in (
                upstream[0],
                signal[0],
                filter_taps,
                skip_gain.reshape(seqs, LANES),
                jnp.asarray(matrices),
                jnp.asarray(twist),
            )
        ]
    )
    input_grad, filter_grad = pl.pallas_call(
        deliver,
        out_shape=[pltpu.HBM(rows, jnp.float32)] * 2,
        in_specs=[vmem] * 2,
        out_specs=[hbm] * 2,
        scratch_shapes=[pltpu.SemaphoreType.DMA((2,))],
    )(*[pltpu.with_memory_space_constraint(part, pltpu.VMEM) for part in parts])
    return (input_grad[None], filter_grad)


def solution(mesh):
    placed = (P("dp", "tp", "ctx"), P("dp", "tp", "ctx"), P("tp", "ctx"), P("tp"))
    return jax.shard_map(
        shards,
        mesh=mesh,
        in_specs=placed,
        out_specs=(P("dp", "tp", "ctx"), P("tp", "ctx")),
        check_vma=False,
    )
```
